128 devices in a mesh: group: 2 (over x_lo), dp: 8 (over z, x_hi), mp: 8 (over y, core).
Axes of the slice: x: 4 (x_hi: 2, x_lo: 2; x = x_hi * 2 + x_lo), y: 4, z: 4, core: 2. Of those that a mesh axis runs over, the one named last changes fastest.
Arguments:
- latent_noise: bfloat16 [8, 768, 2432], P('dp', 'mp'), may hold values from -6 to 6
- timestep: int32 [8], P('dp'), may hold values from 0 to 49
- reward_slot: int32 [8], replicated, may hold values from 0 to 7, each once
- target: bfloat16 [8, 768, 1280], P('dp', 'mp'), may hold values from -6 to 6
- modulation: float32 [50, 3, 2432], replicated, may hold values from -3 to 3
- w_in: bfloat16 [2432, 9728], P(('group', 'dp'), 'mp'), may hold values from -0.125 to 0.125
- w_out_t: bfloat16 [2432, 9728], P(('group', 'dp'), 'mp'), may hold values from -0.0625 to 0.0625
- w_final: bfloat16 [2432, 64], replicated, may hold values from -0.125 to 0.125
- w_dec1: bfloat16 [64, 2048], replicated, may hold values from -0.75 to 0.75
- w_dec2: bfloat16 [2048, 768], replicated, may hold values from -0.125 to 0.125
- w_patch: bfloat16 [768, 1280], replicated, may hold values from -0.21875 to 0.21875
- w_v1: bfloat16 [1280, 5120], P(None, 'mp'), may hold values from -0.15625 to 0.15625
- w_v2: bfloat16 [5120, 1280], P('mp'), may hold values from -0.078125 to 0.078125
Outputs:
- grad_in: float32 [2432, 9728], P(('group', 'dp'), 'mp')
- grad_out_t: float32 [2432, 9728], P(('group', 'dp'), 'mp')
The draws below stay inside these ranges and needn't reach their ends.
Inputs may be any that keep to these rules, and one draw needn't show every extreme that they name: `reward_slot`: each reward slot scores exactly one image.
All inputs are finite; a program needn't handle non-finite values.
Results may differ from the reference program's by a relative error of at most 0.025.
Values may be sent and summed in bfloat16 or wider, within the bound.
No kernel may reach another device: no remote copies, remote signals or barrier semaphores. Data moves between devices by JAX's collectives and lax.ppermute only.
A program may use at most 128 MiB of HBM per device.

```python
import math
import jax
import jax.numpy as jnp
from jax import lax

D = 2432
FF = 9728
LAT = 64
DEC = 2048
PIX = 768
E = 1280
EF = 5120
STEPS = 50
ROWS = 768
IMAGES = 8
N_MP = 8


def touch_ends(entries, key, low, top_value):
    shape = entries.shape
    place = [jax.random.randint(jax.random.fold_in(key, axis), (), 0, shape[axis]) for axis in range(len(shape))]
    entries = entries.at[tuple(place)].set(low)
    longest = shape.index(max(shape))
    place[longest] = (place[longest] + 1) % shape[longest]
    return entries.at[tuple(place)].set(top_value)


def shard_levels(own_key, shape, pieces, low, top_value):
    gain = 1.0
    for axis_at, parts in pieces:
        steps = jax.random.uniform(jax.random.fold_in(jax.random.fold_in(own_key, 6), axis_at), (parts,), jnp.float32, low / len(pieces), top_value / len(pieces))
        gain = gain * jnp.repeat(jnp.exp(steps), shape[axis_at] // parts).reshape((-1,) + (1,) * (len(shape) - 1 - axis_at))
    return gain


def normal_values(own_key, dims, scale, most, split=(), kind=jnp.bfloat16):
    result = scale * jax.random.normal(own_key, dims, jnp.float32)
    if split:
        result = result * shard_levels(own_key, dims, split, -0.22, 0.18)
    return jnp.clip(result, -most, most).astype(kind)


def setup_inputs(seed: int = 0) -> dict:
    key_of = jax.random.split(jax.random.key(seed), 14)
    return {
        "latent_noise": normal_values(key_of[0], (IMAGES, ROWS, D), 1.0, 6.0, ((0, 8), (1, 8))),
        "timestep": touch_ends(jax.random.randint(key_of[1], (IMAGES,), 0, STEPS), jax.random.fold_in(key_of[1], 1), 0, STEPS - 1).astype(jnp.int32),
        "reward_slot": jax.random.permutation(key_of[2], IMAGES).astype(jnp.int32),
        "target": normal_values(key_of[3], (IMAGES, ROWS, E), 1.0, 6.0, ((0, 8), (1, 8))),
        "modulation": normal_values(key_of[4], (STEPS, 3, D), 0.5, 3.0, (), jnp.float32),
        "w_in": normal_values(key_of[5], (D, FF), D ** -0.5, 0.125, ((0, 16), (1, 8))),
        "w_out_t": normal_values(key_of[6], (D, FF), FF ** -0.5, 0.0625, ((0, 16), (1, 8))),
        "w_final": normal_values(key_of[7], (D, LAT), D ** -0.5, 0.125),
        "w_dec1": normal_values(key_of[8], (LAT, DEC), LAT ** -0.5, 0.75),
        "w_dec2": normal_values(key_of[9], (DEC, PIX), DEC ** -0.5, 0.125),
        "w_patch": normal_values(key_of[10], (PIX, E), PIX ** -0.5, 0.21875),
        "w_v1": normal_values(key_of[11], (E, EF), E ** -0.5, 0.15625, ((1, 8),)),
        "w_v2": normal_values(key_of[12], (EF, E), EF ** -0.5, 0.078125, ((0, 8),)),
    }


def layer_norm(values):
    mean = lax.optimization_barrier(jnp.mean(values, axis=-1, keepdims=True))
    centred = values - mean
    variance = lax.optimization_barrier(jnp.mean(centred * centred, axis=-1, keepdims=True))
    return centred * lax.rsqrt(variance + 1e-06)

def gelu_tanh(values):
    return jax.nn.gelu(values, approximate=True)

def gelu_back(values, cotangent):
    _, pullback = jax.vjp(gelu_tanh, values)
    return pullback(cotangent)[0]

def silu_back(values, cotangent):
    _, pullback = jax.vjp(jax.nn.silu, values)
    return pullback(cotangent)[0]

def norm_back(values, cotangent):
    _, pullback = jax.vjp(layer_norm, values)
    return pullback(cotangent)[0]

def rounded(values):
    return lax.optimization_barrier(values.astype(jnp.bfloat16)).astype(jnp.float32)

def matmul(left, right):
    return jnp.dot(left, right, preferred_element_type=jnp.float32)

def grouped_sum(left, right, groups):
    width = left.shape[1] // groups
    total = jnp.zeros((left.shape[0], right.shape[0]), jnp.float32)
    for index in range(groups):
        part = lax.dot_general(left[:, index * width:(index + 1) * width], right[:, index * width:(index + 1) * width], (((1,), (1,)), ((), ())), preferred_element_type=jnp.float32)
        total = total + rounded(part)
    return total

def reference(latent_noise, timestep, reward_slot, target, modulation, w_in, w_out_t, w_final, w_dec1, w_dec2, w_patch, w_v1, w_v2):
    scale = 1.0 / math.sqrt(IMAGES * ROWS)
    matched = jnp.take(target, reward_slot, axis=0)

    def one_image(carry, inputs):
        noise_rows, step_index, goal = inputs
        modulate = modulation[step_index]
        modulated = (layer_norm(noise_rows.astype(jnp.float32)) * (1.0 + modulate[1]) + modulate[0]).astype(jnp.bfloat16)
        pre_act = matmul(modulated, w_in)
        hidden = gelu_tanh(pre_act).astype(jnp.bfloat16)
        block_out = grouped_sum(hidden, w_out_t, N_MP)
        state = (noise_rows.astype(jnp.float32) + modulate[2] * block_out).astype(jnp.bfloat16)
        latent = matmul(state, w_final).astype(jnp.bfloat16)
        dec_pre = matmul(latent, w_dec1)
        dec_act = jax.nn.silu(dec_pre).astype(jnp.bfloat16)
        pixels = matmul(dec_act, w_dec2).astype(jnp.bfloat16)
        embedded = matmul(pixels, w_patch)
        normed_patch = layer_norm(embedded).astype(jnp.bfloat16)
        vit_pre = matmul(normed_patch, w_v1)
        vit_hidden = gelu_tanh(vit_pre).astype(jnp.bfloat16)
        vit_out = grouped_sum(vit_hidden, w_v2.T, N_MP)
        features = embedded + vit_out
        feature_grad = ((features - goal.astype(jnp.float32)) * scale).astype(jnp.bfloat16)
        vit_hidden_grad = matmul(feature_grad, w_v2.T)
        vit_pre_grad = gelu_back(vit_pre, vit_hidden_grad).astype(jnp.bfloat16)
        norm_grad = grouped_sum(vit_pre_grad, w_v1, N_MP)
        embed_grad = (feature_grad.astype(jnp.float32) + norm_back(embedded, norm_grad)).astype(jnp.bfloat16)
        pixel_grad = matmul(embed_grad, w_patch.T).astype(jnp.bfloat16)
        decode_grad = matmul(pixel_grad, w_dec2.T)
        dec_pre_grad = silu_back(dec_pre, decode_grad).astype(jnp.bfloat16)
        latent_grad = matmul(dec_pre_grad, w_dec1.T).astype(jnp.bfloat16)
        state_grad = matmul(latent_grad, w_final.T)
        block_grad = (modulate[2] * state_grad).astype(jnp.bfloat16)
        hidden_grad = matmul(block_grad, w_out_t)
        pre_grad = gelu_back(pre_act, hidden_grad).astype(jnp.bfloat16)
        term_in = matmul(modulated.T, pre_grad)
        term_out = matmul(block_grad.T, hidden)
        return ((carry[0] + rounded(term_in), carry[1] + rounded(term_out)), None)
    start = (jnp.zeros((D, FF), jnp.float32), jnp.zeros((D, FF), jnp.float32))
    (grad_in, grad_out_t), _ = lax.scan(one_image, start, (latent_noise, timestep.astype(jnp.int32), matched))
    return (grad_in, grad_out_t)
```

```python
import math

import jax
import jax.numpy as jnp
from jax import lax
from jax.sharding import Mesh
from jax.sharding import PartitionSpec as P

BF16 = jnp.bfloat16
F32 = jnp.float32
AXES = ("near", "z", "far", "y", "core")
IMAGE = ("z", "far")
ROWS_AT = ("near", "z", "far")
TOKENS_AT = ("near", "y", "core")


def layer_norm(values):
    mean = jnp.mean(values, axis=-1, keepdims=True)
    centred = values - mean
    variance = jnp.mean(centred * centred, axis=-1, keepdims=True)
    return centred * lax.rsqrt(variance + 1e-06)


def gelu_tanh(values):
    return jax.nn.gelu(values, approximate=True)


def with_slope(function, values):
    result, pullback = jax.vjp(function, values)
    return result, pullback(jnp.ones_like(values))[0]


def norm_back(values, cotangent):
    _, pullback = jax.vjp(layer_norm, values)
    return pullback(cotangent)[0]


def matmul(left, right):
    return jnp.dot(left, right, preferred_element_type=F32)


def matmul_nt(left, right):
    return lax.dot_general(left, right, (((1,), (1,)), ((), ())), preferred_element_type=F32)


def matmul_tn(left, right):
    return lax.dot_general(left, right, (((0,), (0,)), ((), ())), preferred_element_type=F32)


def turned(value, axis, steps):
    count = lax.axis_size(axis)
    return lax.ppermute(value, axis, [(at, (at + steps) % count) for at in range(count)])


def from_all(value, axis):
    count = lax.axis_size(axis)
    return [value] + [turned(value, axis, step) for step in range(1, count)]


def summed_back(blocks, axis):
    total = blocks[0]
    for step in range(1, len(blocks)):
        total = total + turned(blocks[step].astype(BF16), axis, -step).astype(F32)
    return total


def exchanged(blocks, axis):
    return lax.all_to_all(blocks, axis, 0, 0, tiled=True)


def on_device(
    latent_noise,
    timestep,
    reward_slot,
    target,
    modulation,
    w_in,
    w_out_t,
    w_final,
    w_dec1,
    w_dec2,
    w_patch,
    w_v1,
    w_v2,
):
    tok_dev = latent_noise.shape[1]
    n_near, n_y, n_core = (lax.axis_size(axis) for axis in TOKENS_AT)
    n_images = lax.axis_size("z") * lax.axis_size("far")
    n_rows = n_near * n_images
    n_tokens = n_near * n_y * n_core
    mine = tok_dev // n_near
    rows = tok_dev * n_y * n_core
    d_dev, ff_mp = w_in.shape
    width_d = d_dev * n_rows
    half = ff_mp // n_near
    strip = ff_mp // n_rows
    lat = w_final.shape[1]
    scale = 1.0 / math.sqrt(n_images * rows)
    near = lax.axis_index("near")
    my_image = lax.axis_index(IMAGE)
    my_slot = reward_slot[my_image]

    split_in = jnp.moveaxis(w_in.reshape(d_dev, n_near, half), 1, 0)
    keep = lax.dynamic_index_in_dim(split_in, near, 0, keepdims=False)
    give = lax.dynamic_index_in_dim(split_in, 1 - near, 0, keepdims=False)
    got = turned(give, "near", 1)
    pair = jnp.stack([jnp.where(near == 0, keep, got), jnp.where(near == 0, got, keep)])
    full_in = jnp.zeros((n_near, n_images, d_dev, half), BF16)
    for step, block in enumerate(from_all(pair, IMAGE)):
        owner = (my_image - step) % n_images
        full_in = lax.dynamic_update_slice_in_dim(full_in, block[:, None], owner, 1)
    full_in = full_in.reshape(width_d, half)

    modulate = modulation[timestep[0]]
    noise_rows = latent_noise[0]
    modulated = (
        layer_norm(noise_rows.astype(F32)) * (1.0 + modulate[1]) + modulate[0]
    ).astype(BF16)
    token_rows = lax.all_gather(modulated, ("y", "core"), axis=0, tiled=True)

    strips = jnp.moveaxis(w_out_t.reshape(d_dev, n_rows, strip), 1, 0)
    steps_row = jnp.broadcast_to(timestep[0].astype(BF16), (n_rows, 8, strip))
    arrived = exchanged(jnp.concatenate([strips, steps_row], axis=1), ROWS_AT)
    strip_rows = arrived[:, :d_dev].reshape(width_d, strip)
    all_steps = arrived[:n_images, d_dev, 0].astype(jnp.int32)
    gates = modulation[all_steps, 2]
    gated_final = (gates.T[:, :, None] * w_final.astype(F32)[:, None, :]).astype(BF16)
    gated_final = gated_final.reshape(width_d, n_images * lat)
    through = matmul_tn(strip_rows, gated_final).astype(BF16)
    through = exchanged(jnp.moveaxis(through.reshape(strip, n_images, lat), 1, 0), IMAGE)
    through = through.reshape(half, lat)

    v1_both = (w_v1, turned(w_v1, "core", 1))
    v2_both = (w_v2, turned(w_v2, "core", 1))
    my_target = lax.dynamic_slice_in_dim(target[0], near * mine, mine, 0)
    goals = lax.all_gather(my_target, IMAGE, axis=0)
    goal = lax.dynamic_index_in_dim(goals, my_slot, 0, keepdims=False).astype(F32)

    pre_act = matmul(token_rows, full_in)
    hidden, hidden_slope = with_slope(gelu_tanh, pre_act)
    hidden = hidden.astype(BF16)
    latent_part = matmul(hidden, through)
    latent_part = jnp.moveaxis(latent_part.reshape(n_y * n_core, n_near, mine, lat), 1, 0)
    latent_parts = exchanged(latent_part.reshape(n_tokens, mine, lat), TOKENS_AT)
    my_noise = lax.dynamic_slice_in_dim(noise_rows, near * mine, mine, 0)
    latent = (matmul(my_noise, w_final) + jnp.sum(latent_parts, axis=0)).astype(BF16)

    dec_pre = matmul(latent, w_dec1)
    dec_act, dec_slope = with_slope(jax.nn.silu, dec_pre)
    pixels = matmul(dec_act.astype(BF16), w_dec2).astype(BF16)
    embedded = matmul(pixels, w_patch)
    normed = layer_norm(embedded).astype(BF16)

    patch_rows = jnp.concatenate(from_all(normed, "y"))
    slopes = []
    vit_part = 0.0
    for v1, v2 in zip(v1_both, v2_both):
        act, slope = with_slope(gelu_tanh, matmul(patch_rows, v1))
        slopes.append(slope)
        vit_part = vit_part + matmul(act.astype(BF16), v2)
    vit_out = summed_back(jnp.split(vit_part, n_y), "y")
    feature_grad = ((embedded + vit_out - goal) * scale).astype(BF16)

    grad_rows = jnp.concatenate(from_all(feature_grad, "y"))
    norm_part = 0.0
    for v1, v2, slope in zip(v1_both, v2_both, slopes):
        vit_pre_grad = (slope * matmul_nt(grad_rows, v2)).astype(BF16)
        norm_part = norm_part + matmul_nt(vit_pre_grad, v1)
    norm_grad = summed_back(jnp.split(norm_part, n_y), "y")
    embed_grad = (feature_grad.astype(F32) + norm_back(embedded, norm_grad)).astype(BF16)
    pixel_grad = matmul_nt(embed_grad, w_patch).astype(BF16)
    dec_pre_grad = (dec_slope * matmul_nt(pixel_grad, w_dec2)).astype(BF16)
    latent_grad = matmul_nt(dec_pre_grad, w_dec1).astype(BF16)

    spread = jnp.broadcast_to(latent_grad, (n_tokens, mine, lat))
    latent_rows = exchanged(spread, TOKENS_AT).reshape(n_near, n_y * n_core, mine, lat)
    latent_rows = jnp.moveaxis(latent_rows, 0, 1).reshape(rows, lat)

    inner = matmul_tn(latent_rows, hidden).astype(BF16)
    inner = exchanged(jnp.moveaxis(inner.reshape(lat, n_images, strip), 1, 0), IMAGE)
    out_strip = matmul(gated_final, inner.reshape(n_images * lat, strip)).astype(BF16)
    out_strips = exchanged(out_strip.reshape(n_rows, d_dev, strip), ROWS_AT)
    grad_out_t = jnp.moveaxis(out_strips, 0, 1).reshape(d_dev, ff_mp).astype(F32)

    pre_grad = (hidden_slope * matmul_nt(latent_rows, through)).astype(BF16)
    term_in = matmul_tn(token_rows, pre_grad).astype(BF16)
    terms = exchanged(term_in.reshape(n_rows, d_dev, half), ROWS_AT)
    grad_in = jnp.sum(terms.reshape(n_near, n_images, d_dev, half).astype(F32), axis=1)
    grad_in = jnp.moveaxis(grad_in, 0, 1).reshape(d_dev, ff_mp)
    return (grad_in, grad_out_t)


def solution(mesh):
    n_group, n_dp, n_mp = (mesh.shape[axis] for axis in ("group", "dp", "mp"))
    fine = Mesh(mesh.devices.reshape(n_group, n_dp // 2, 2, n_mp // 2, 2), AXES)
    tokens = ("y", "core")
    weights = P(ROWS_AT, tokens)
    placed = (
        P(IMAGE, tokens, None),
        P(IMAGE),
        P(),
        P(IMAGE, tokens, None),
        P(),
        weights,
        weights,
        P(),
        P(),
        P(),
        P(),
        P(None, tokens),
        P(tokens, None),
    )
    return jax.shard_map(
        on_device, mesh=fine, in_specs=placed, out_specs=(weights, weights), check_vma=False
    )
```

```python
import math

import jax
import jax.numpy as jnp
from jax import lax
from jax.sharding import Mesh
from jax.sharding import PartitionSpec as P

BF16 = jnp.bfloat16
F32 = jnp.float32
AXES = ("near", "z", "far", "y", "core")
IMAGE = ("z", "far")
ROWS_AT = ("near", "z", "far")
TOKENS_AT = ("near", "y", "core")


def layer_norm(values):
    mean = jnp.mean(values, axis=-1, keepdims=True)
    centred = values - mean
    variance = jnp.mean(centred * centred, axis=-1, keepdims=True)
    return centred * lax.rsqrt(variance + 1e-06)


def gelu_tanh(values):
    return jax.nn.gelu(values, approximate=True)


def with_slope(function, values):
    result, pullback = jax.vjp(function, values)
    return result, pullback(jnp.ones_like(values))[0]


def norm_back(values, cotangent):
    _, pullback = jax.vjp(layer_norm, values)
    return pullback(cotangent)[0]


def matmul(left, right):
    return jnp.dot(left, right, preferred_element_type=F32)


def matmul_nt(left, right):
    return lax.dot_general(left, right, (((1,), (1,)), ((), ())), preferred_element_type=F32)


def matmul_tn(left, right):
    return lax.dot_general(left, right, (((0,), (0,)), ((), ())), preferred_element_type=F32)


def turned(value, axis, steps):
    count = lax.axis_size(axis)
    return lax.ppermute(value, axis, [(at, (at + steps) % count) for at in range(count)])


def from_all(value, axis):
    count = lax.axis_size(axis)
    return [value] + [turned(value, axis, step) for step in range(1, count)]


def summed_back(blocks, axis):
    total = blocks[0]
    for step in range(1, len(blocks)):
        total = total + turned(blocks[step].astype(BF16), axis, -step).astype(F32)
    return total


def exchanged(blocks, axis):
    return lax.all_to_all(blocks, axis, 0, 0, tiled=True)


def on_device(
    latent_noise,
    timestep,
    reward_slot,
    target,
    modulation,
    w_in,
    w_out_t,
    w_final,
    w_dec1,
    w_dec2,
    w_patch,
    w_v1,
    w_v2,
):
    tok_dev = latent_noise.shape[1]
    n_near, n_y, n_core = (lax.axis_size(axis) for axis in TOKENS_AT)
    n_images = lax.axis_size("z") * lax.axis_size("far")
    n_rows = n_near * n_images
    n_tokens = n_near * n_y * n_core
    mine = tok_dev // n_near
    rows = tok_dev * n_y * n_core
    d_dev, ff_mp = w_in.shape
    width_d = d_dev * n_rows
    half = ff_mp // n_near
    strip = ff_mp // n_rows
    lat = w_final.shape[1]
    scale = 1.0 / math.sqrt(n_images * rows)
    near = lax.axis_index("near")
    my_image = lax.axis_index(IMAGE)
    my_slot = reward_slot[my_image]

    split_in = jnp.moveaxis(w_in.reshape(d_dev, n_near, half), 1, 0)
    split_in = jnp.broadcast_to(split_in[:, None], (n_near, n_images, d_dev, half))
    full_in = exchanged(split_in.reshape(n_rows, d_dev, half), ROWS_AT).reshape(width_d, half)

    modulate = modulation[timestep[0]]
    noise_rows = latent_noise[0]
    modulated = (
        layer_norm(noise_rows.astype(F32)) * (1.0 + modulate[1]) + modulate[0]
    ).astype(BF16)
    token_rows = lax.all_gather(modulated, ("y", "core"), axis=0, tiled=True)

    strips = jnp.moveaxis(w_out_t.reshape(d_dev, n_rows, strip), 1, 0)
    steps_row = jnp.broadcast_to(timestep[0].astype(BF16), (n_rows, 8, strip))
    arrived = exchanged(jnp.concatenate([strips, steps_row], axis=1), ROWS_AT)
    strip_rows = arrived[:, :d_dev].reshape(width_d, strip)
    all_steps = arrived[:n_images, d_dev, 0].astype(jnp.int32)
    gates = modulation[all_steps, 2]
    gated_final = (gates.T[:, :, None] * w_final.astype(F32)[:, None, :]).astype(BF16)
    gated_final = gated_final.reshape(width_d, n_images * lat)
    through = matmul_tn(strip_rows, gated_final).astype(BF16)
    through = jnp.moveaxis(through.reshape(strip, n_images, lat), 1, 0)
    through, full_in = lax.optimization_barrier((through, full_in))
    through = exchanged(through, IMAGE).reshape(half, lat)

    v1_both = (w_v1, turned(w_v1, "core", 1))
    v2_both = (w_v2, turned(w_v2, "core", 1))
    my_target = lax.dynamic_slice_in_dim(target[0], near * mine, mine, 0)

    pre_act = matmul(token_rows, full_in)
    hidden, hidden_slope = with_slope(gelu_tanh, pre_act)
    hidden = hidden.astype(BF16)
    n_mp = n_y * n_core
    own_part = matmul(noise_rows, w_final).reshape(1, n_near, mine, lat)
    here = (lax.iota(jnp.int32, n_mp) == lax.axis_index(("y", "core")))[:, None]
    here = here & (lax.iota(jnp.int32, n_near) == near)[None]
    latent_part = matmul(hidden, through).reshape(n_mp, n_near, mine, lat)
    latent_part = (latent_part + jnp.where(here[:, :, None, None], own_part, 0.0)).astype(BF16)
    my_target, latent_part = lax.optimization_barrier((my_target, latent_part))
    latent_part = latent_part.reshape(n_y, n_core, n_near, mine, lat).transpose(2, 1, 0, 3, 4)
    latent_part = jnp.broadcast_to(latent_part[:, None], (n_near, n_y) + latent_part.shape[1:])
    latent_parts = exchanged(latent_part.reshape(n_tokens, n_y * mine, lat), TOKENS_AT)
    latents = jnp.sum(latent_parts.astype(F32), axis=0).astype(BF16)
    goals = exchanged(jnp.broadcast_to(my_target, (n_images,) + my_target.shape), IMAGE)
    goal = lax.dynamic_index_in_dim(goals, my_slot, 0, keepdims=False).astype(F32)
    my_y = lax.axis_index("y")
    latent = jnp.concatenate(
        [
            lax.dynamic_slice_in_dim(latents, (my_y - step) % n_y * mine, mine, 0)
            for step in range(n_y)
        ]
    )

    dec_pre = matmul(latent, w_dec1)
    dec_act, dec_slope = with_slope(jax.nn.silu, dec_pre)
    pixels = matmul(dec_act.astype(BF16), w_dec2).astype(BF16)
    embedded = matmul(pixels, w_patch)
    patch_rows = layer_norm(embedded).astype(BF16)
    embedded = embedded[:mine]
    dec_slope = dec_slope[:mine]

    slopes = []
    vit_part = 0.0
    for v1, v2 in zip(v1_both, v2_both):
        act, slope = with_slope(gelu_tanh, matmul(patch_rows, v1))
        slopes.append(slope)
        vit_part = vit_part + matmul(act.astype(BF16), v2)
    vit_out = summed_back(jnp.split(vit_part, n_y), "y")
    feature_grad = ((embedded + vit_out - goal) * scale).astype(BF16)

    grad_rows = jnp.concatenate(from_all(feature_grad, "y"))
    norm_part = 0.0
    for v1, v2, slope in zip(v1_both, v2_both, slopes):
        vit_pre_grad = (slope * matmul_nt(grad_rows, v2)).astype(BF16)
        norm_part = norm_part + matmul_nt(vit_pre_grad, v1)
    norm_grad = summed_back(jnp.split(norm_part, n_y), "y")
    embed_grad = (feature_grad.astype(F32) + norm_back(embedded, norm_grad)).astype(BF16)
    pixel_grad = matmul_nt(embed_grad, w_patch).astype(BF16)
    dec_pre_grad = (dec_slope * matmul_nt(pixel_grad, w_dec2)).astype(BF16)
    latent_grad = matmul_nt(dec_pre_grad, w_dec1).astype(BF16)

    spread = jnp.broadcast_to(latent_grad, (n_tokens, mine, lat))
    latent_rows = exchanged(spread, TOKENS_AT).reshape(n_near, n_y * n_core, mine, lat)
    latent_rows = jnp.moveaxis(latent_rows, 0, 1).reshape(rows, lat)

    pre_grad = (hidden_slope * matmul_nt(latent_rows, through)).astype(BF16)
    term_in = matmul_tn(token_rows, pre_grad).astype(BF16)
    terms = exchanged(term_in.reshape(n_rows, d_dev, half), ROWS_AT)
    grad_in = jnp.sum(terms.reshape(n_near, n_images, d_dev, half).astype(F32), axis=1)
    grad_in = jnp.moveaxis(grad_in, 0, 1).reshape(d_dev, ff_mp)

    inner = matmul_tn(latent_rows, hidden).astype(BF16)
    inner = exchanged(jnp.moveaxis(inner.reshape(lat, n_images, strip), 1, 0), IMAGE)
    out_strip = matmul(gated_final, inner.reshape(n_images * lat, strip)).astype(BF16)
    out_strips = exchanged(out_strip.reshape(n_rows, d_dev, strip), ROWS_AT)
    grad_out_t = jnp.moveaxis(out_strips, 0, 1).reshape(d_dev, ff_mp).astype(F32)
    return (grad_in, grad_out_t)


def solution(mesh):
    n_group, n_dp, n_mp = (mesh.shape[axis] for axis in ("group", "dp", "mp"))
    fine = Mesh(mesh.devices.reshape(n_group, n_dp // 2, 2, n_mp // 2, 2), AXES)
    tokens = ("y", "core")
    weights = P(ROWS_AT, tokens)
    placed = (
        P(IMAGE, tokens, None),
        P(IMAGE),
        P(),
        P(IMAGE, tokens, None),
        P(),
        weights,
        weights,
        P(),
        P(),
        P(),
        P(),
        P(None, tokens),
        P(tokens, None),
    )
    return jax.shard_map(
        on_device, mesh=fine, in_specs=placed, out_specs=(weights, weights), check_vma=False
    )
```

```python
import math

import jax
import jax.numpy as jnp
from jax import lax
from jax.experimental import pallas as pl
from jax.experimental.pallas import tpu as pltpu
from jax.sharding import Mesh
from jax.sharding import PartitionSpec as P

BF16 = jnp.bfloat16
GELU_SCALE = math.sqrt(2.0 / math.pi)
VMEM_BYTES = 56 * 1024 * 1024
F32 = jnp.float32
AXES = ("near", "z", "far", "y", "core")
IMAGE = ("z", "far")
ROWS_AT = ("near", "z", "far")
TOKENS_AT = ("near", "y", "core")


def layer_norm(values):
    mean = jnp.mean(values, axis=-1, keepdims=True)
    centred = values - mean
    variance = jnp.mean(centred * centred, axis=-1, keepdims=True)
    return centred * lax.rsqrt(variance + 1e-06)


def gelu_and_slope(values):
    inner = GELU_SCALE * (values + 0.044715 * values * values * values)
    bent = jnp.tanh(inner)
    half = 0.5 * (1.0 + bent)
    rate = GELU_SCALE * (1.0 + 3 * 0.044715 * values * values)
    return values * half, half + 0.5 * values * (1.0 - bent * bent) * rate


def silu_and_slope(values):
    gate = jax.nn.sigmoid(values)
    result = values * gate
    return result, gate + result * (1.0 - gate)


def norm_back(values, cotangent):
    _, pullback = jax.vjp(layer_norm, values)
    return pullback(cotangent)[0]


def matmul(left, right):
    return jnp.dot(left, right, preferred_element_type=F32)


def matmul_nt(left, right):
    return lax.dot_general(left, right, (((1,), (1,)), ((), ())), preferred_element_type=F32)


def matmul_tn(left, right):
    return lax.dot_general(left, right, (((0,), (0,)), ((), ())), preferred_element_type=F32)


def turned(value, axis, steps):
    count = lax.axis_size(axis)
    return lax.ppermute(value, axis, [(at, (at + steps) % count) for at in range(count)])


def from_all(value, axis):
    count = lax.axis_size(axis)
    return [value] + [turned(value, axis, step) for step in range(1, count)]


def summed_back(blocks, axis):
    total = blocks[0].astype(F32)
    for step in range(1, len(blocks)):
        total = total + turned(blocks[step], axis, -step).astype(F32)
    return total


def by_turns(blocks, axis):
    count = lax.axis_size(axis)
    here = lax.axis_index(axis)
    blocks = lax.optimization_barrier(blocks)
    result = []
    for step in range(count):
        block = lax.dynamic_slice_in_dim(blocks, (here + step) % count, 1, 0)
        result.append(turned(block, axis, step) if step else block)
    return result


def exchanged(blocks, axis):
    return lax.all_to_all(blocks, axis, 0, 0, tiled=True)


def whole(array):
    return pl.BlockSpec(array.shape, lambda step: (0,) * len(array.shape))


def call(kernel, grid, in_specs, out_specs, out_shape, scratch, flops, moved, *operands):
    return pl.pallas_call(
        kernel,
        grid=(grid,),
        in_specs=in_specs,
        out_specs=out_specs,
        out_shape=out_shape,
        scratch_shapes=scratch,
        compiler_params=pltpu.CompilerParams(vmem_limit_bytes=VMEM_BYTES),
        cost_estimate=pl.CostEstimate(flops=flops, bytes_accessed=moved, transcendentals=0),
    )(*operands)


def block_forward_kernel(tokens, weights, through, hidden, slope, latent):
    act, rate = gelu_and_slope(matmul(tokens[...], weights[...]))
    act = act.astype(BF16)
    hidden[...] = act
    slope[...] = rate.astype(BF16)
    latent[...] = matmul(act, through[...])


def block_forward(tokens, weights, through):
    rows, width = tokens.shape
    columns, lat = through.shape
    tile = rows // 4
    by_rows = lambda last: pl.BlockSpec((tile, last), lambda step: (step, 0))
    return call(
        block_forward_kernel,
        4,
        [by_rows(width), whole(weights), whole(through)],
        [by_rows(columns), by_rows(columns), by_rows(lat)],
        [
            jax.ShapeDtypeStruct((rows, columns), BF16),
            jax.ShapeDtypeStruct((rows, columns), BF16),
            jax.ShapeDtypeStruct((rows, lat), F32),
        ],
        [],
        2 * rows * columns * width,
        2 * (rows * width + width * columns + 2 * rows * columns),
        tokens,
        weights,
        through,
    )


def block_backward_kernel(latent_grad, through, slope, tokens, term, pre_grad):
    @pl.when(pl.program_id(0) == 0)
    def _():
        back = matmul_nt(latent_grad[...], through[...])
        pre_grad[...] = (slope[...].astype(F32) * back).astype(BF16)

    term[...] = matmul_tn(tokens[...], pre_grad[...]).astype(BF16)


def block_backward(latent_grad, through, slope, tokens):
    rows, width = tokens.shape
    columns = slope.shape[1]
    tile = min(640, width)
    return call(
        block_backward_kernel,
        pl.cdiv(width, tile),
        [
            whole(latent_grad),
            whole(through),
            whole(slope),
            pl.BlockSpec((rows, tile), lambda step: (0, step)),
        ],
        pl.BlockSpec((tile, columns), lambda step: (step, 0)),
        jax.ShapeDtypeStruct((width, columns), BF16),
        [pltpu.VMEM((rows, columns), BF16)],
        2 * rows * columns * width,
        2 * (rows * width + width * columns + rows * columns),
        latent_grad,
        through,
        slope,
        tokens,
    )


def decode_kernel(latent, w_dec1, w_dec2, w_patch, normed, embedded, slope, pixels):
    step = pl.program_id(0)
    act, rate = silu_and_slope(matmul(latent[...], w_dec1[...]))
    slope[...] = rate[: slope.shape[0]]
    part = matmul(act.astype(BF16), w_dec2[...])

    @pl.when(step == 0)
    def _():
        pixels[...] = part

    @pl.when(step > 0)
    def _():
        pixels[...] += part

    @pl.when(step == pl.num_programs(0) - 1)
    def _():
        patches = matmul(pixels[...].astype(BF16), w_patch[...])
        normed[...] = layer_norm(patches).astype(BF16)
        embedded[...] = patches[: embedded.shape[0]]


def decode(latent, w_dec1, w_dec2, w_patch, mine):
    rows, lat = latent.shape
    deep, pix = w_dec2.shape
    width = w_patch.shape[1]
    tile = min(512, deep)
    return call(
        decode_kernel,
        deep // tile,
        [
            whole(latent),
            pl.BlockSpec((lat, tile), lambda step: (0, step)),
            pl.BlockSpec((tile, pix), lambda step: (step, 0)),
            whole(w_patch),
        ],
        [
            pl.BlockSpec((rows, width), lambda step: (0, 0)),
            pl.BlockSpec((mine, width), lambda step: (0, 0)),
            pl.BlockSpec((mine, tile), lambda step: (0, step)),
        ],
        [
            jax.ShapeDtypeStruct((rows, width), BF16),
            jax.ShapeDtypeStruct((mine, width), F32),
            jax.ShapeDtypeStruct((mine, deep), F32),
        ],
        [pltpu.VMEM((rows, pix), F32)],
        2 * rows * (lat * deep + deep * pix + pix * width),
        2 * (deep * pix + pix * width),
        latent,
        w_dec1,
        w_dec2,
        w_patch,
    )


def reward_forward_kernel(normed, v1a, v1b, v2a, v2b, slope_a, slope_b, out, total):
    step = pl.program_id(0)
    part = 0.0
    for v1, v2, slope in ((v1a, v2a, slope_a), (v1b, v2b, slope_b)):
        act, rate = gelu_and_slope(matmul(normed[...], v1[...]))
        slope[...] = rate
        part = part + matmul(act.astype(BF16), v2[...])

    @pl.when(step == 0)
    def _():
        total[...] = part

    @pl.when(step > 0)
    def _():
        total[...] += part

    @pl.when(step == pl.num_programs(0) - 1)
    def _():
        out[...] = total[...].astype(BF16)


def reward_backward_kernel(grad, v1a, v1b, v2a, v2b, slope_a, slope_b, out, total):
    step = pl.program_id(0)
    part = 0.0
    for v1, v2, slope in ((v1a, v2a, slope_a), (v1b, v2b, slope_b)):
        back = (slope[...] * matmul_nt(grad[...], v2[...])).astype(BF16)
        part = part + matmul_nt(back, v1[...])

    @pl.when(step == 0)
    def _():
        total[...] = part

    @pl.when(step > 0)
    def _():
        total[...] += part

    @pl.when(step == pl.num_programs(0) - 1)
    def _():
        out[...] = total[...].astype(BF16)


def reward(values, v1_both, v2_both, slopes=None):
    rows, width = values.shape
    hidden = v1_both[0].shape[1]
    tile = min(128, hidden)
    slope_spec = pl.BlockSpec((rows, tile), lambda step: (0, step))
    slope_shape = jax.ShapeDtypeStruct((rows, hidden), F32)
    out_spec = pl.BlockSpec((rows, width), lambda step: (0, 0))
    out_shape = jax.ShapeDtypeStruct((rows, width), BF16)
    v1_spec = pl.BlockSpec((width, tile), lambda step: (0, step))
    v2_spec = pl.BlockSpec((tile, width), lambda step: (step, 0))
    weight_specs = [whole(values), v1_spec, v1_spec, v2_spec, v2_spec]
    forward = slopes is None
    return call(
        reward_forward_kernel if forward else reward_backward_kernel,
        hidden // tile,
        weight_specs + ([] if forward else [slope_spec] * 2),
        [slope_spec] * 2 + [out_spec] if forward else out_spec,
        [slope_shape] * 2 + [out_shape] if forward else out_shape,
        [pltpu.VMEM((rows, width), F32)],
        8 * rows * width * hidden,
        8 * width * hidden,
        values,
        *v1_both,
        *v2_both,
        *(() if forward else slopes),
    )


def on_device(
    latent_noise,
    timestep,
    reward_slot,
    target,
    modulation,
    w_in,
    w_out_t,
    w_final,
    w_dec1,
    w_dec2,
    w_patch,
    w_v1,
    w_v2,
):
    tok_dev = latent_noise.shape[1]
    n_near, n_y, n_core = (lax.axis_size(axis) for axis in TOKENS_AT)
    n_images = lax.axis_size("z") * lax.axis_size("far")
    n_rows = n_near * n_images
    n_tokens = n_near * n_y * n_core
    mine = tok_dev // n_near
    rows = tok_dev * n_y * n_core
    d_dev, ff_mp = w_in.shape
    width_d = d_dev * n_rows
    half = ff_mp // n_near
    strip = ff_mp // n_rows
    lat = w_final.shape[1]
    scale = 1.0 / math.sqrt(n_images * rows)
    near = lax.axis_index("near")
    my_image = lax.axis_index(IMAGE)
    my_slot = reward_slot[my_image]

    strips = jnp.moveaxis(w_out_t.reshape(d_dev, n_rows, strip), 1, 0)
    steps_row = jnp.broadcast_to(timestep[0].astype(BF16), (n_rows, 8, strip))
    strips = jnp.concatenate([strips, steps_row], axis=1)
    split_in = jnp.moveaxis(w_in.reshape(d_dev, n_near, half), 1, 0)
    split_in = jnp.broadcast_to(split_in[:, None], (n_near, n_images, d_dev, half))
    split_in = split_in.reshape(n_rows, d_dev, half)
    strips, split_in = lax.optimization_barrier((strips, split_in))
    arrived = exchanged(strips, ROWS_AT)
    arrived, split_in, noise_rows = lax.optimization_barrier((arrived, split_in, latent_noise[0]))
    full_in = exchanged(split_in, ROWS_AT).reshape(width_d, half)

    modulate = modulation[timestep[0]]
    modulated = (
        layer_norm(noise_rows.astype(F32)) * (1.0 + modulate[1]) + modulate[0]
    ).astype(BF16)
    token_rows = lax.all_gather(modulated, ("y", "core"), axis=0, tiled=True)

    strip_rows = arrived[:, :d_dev].reshape(width_d, strip)
    all_steps = arrived[:n_images, d_dev, 0].astype(jnp.int32)
    gates = modulation[all_steps, 2]
    gated_final = (gates.T[:, :, None] * w_final.astype(F32)[:, None, :]).astype(BF16)
    gated_final = gated_final.reshape(width_d, n_images * lat)
    through = matmul_tn(strip_rows, gated_final).astype(BF16)
    through = jnp.moveaxis(through.reshape(strip, n_images, lat), 1, 0)
    turns = by_turns(through, IMAGE)
    through = jnp.zeros_like(through)
    for step, block in enumerate(turns):
        owner = (my_image - step) % n_images
        through = lax.dynamic_update_slice_in_dim(through, block, owner, 0)
    through = through.reshape(half, lat)

    v1_both = (w_v1, turned(w_v1, "core", 1))
    v2_both = (w_v2, turned(w_v2, "core", 1))
    my_target = lax.dynamic_slice_in_dim(target[0], near * mine, mine, 0)

    hidden, hidden_slope, latent_part = block_forward(token_rows, full_in, through)
    n_mp = n_y * n_core
    own_part = matmul(noise_rows, w_final).reshape(1, n_near, mine, lat)
    here = (lax.iota(jnp.int32, n_mp) == lax.axis_index(("y", "core")))[:, None]
    here = here & (lax.iota(jnp.int32, n_near) == near)[None]
    latent_part = latent_part.reshape(n_mp, n_near, mine, lat)
    latent_part = (latent_part + jnp.where(here[:, :, None, None], own_part, 0.0)).astype(BF16)
    my_target, latent_part = lax.optimization_barrier((my_target, latent_part))
    latent_part = latent_part.reshape(n_y, n_core, n_near, mine, lat).transpose(2, 1, 0, 3, 4)
    latent_part = jnp.broadcast_to(latent_part[:, None], (n_near, n_y) + latent_part.shape[1:])
    latent_parts = exchanged(latent_part.reshape(n_tokens, n_y * mine, lat), TOKENS_AT)
    latents = jnp.sum(latent_parts.astype(F32), axis=0).astype(BF16)
    goals = exchanged(jnp.broadcast_to(my_target, (n_images,) + my_target.shape), IMAGE)
    goal = lax.dynamic_index_in_dim(goals, my_slot, 0, keepdims=False).astype(F32)
    my_y = lax.axis_index("y")
    latent = jnp.concatenate(
        [
            lax.dynamic_slice_in_dim(latents, (my_y - step) % n_y * mine, mine, 0)
            for step in range(n_y)
        ]
    )

    patch_rows, embedded, dec_slope = decode(latent, w_dec1, w_dec2, w_patch, mine)
    *slopes, vit_part = reward(patch_rows, v1_both, v2_both)
    vit_out = summed_back(jnp.split(vit_part, n_y), "y")
    feature_grad = ((embedded + vit_out - goal) * scale).astype(BF16)

    grad_rows = jnp.concatenate(from_all(feature_grad, "y"))
    norm_part = reward(grad_rows, v1_both, v2_both, slopes)
    norm_grad = summed_back(jnp.split(norm_part, n_y), "y")
    embed_grad = (feature_grad.astype(F32) + norm_back(embedded, norm_grad)).astype(BF16)
    pixel_grad = matmul_nt(embed_grad, w_patch).astype(BF16)
    dec_pre_grad = (dec_slope * matmul_nt(pixel_grad, w_dec2)).astype(BF16)
    latent_grad = matmul_nt(dec_pre_grad, w_dec1).astype(BF16)

    spread = jnp.broadcast_to(latent_grad, (n_tokens, mine, lat))
    latent_rows = exchanged(spread, TOKENS_AT).reshape(n_near, n_y * n_core, mine, lat)
    latent_rows = jnp.moveaxis(latent_rows, 0, 1).reshape(rows, lat)

    term_in = block_backward(latent_rows, through, hidden_slope, token_rows)
    term_in, latent_rows = lax.optimization_barrier((term_in, latent_rows))
    terms = exchanged(term_in.reshape(n_rows, d_dev, half), ROWS_AT)

    inner = matmul_tn(latent_rows, hidden).astype(BF16)
    inner = by_turns(jnp.moveaxis(inner.reshape(lat, n_images, strip), 1, 0), IMAGE)
    inner = jnp.concatenate(inner).reshape(n_images * lat, strip)
    turned_gates = jnp.concatenate(
        [
            lax.dynamic_slice_in_dim(gates, (my_image - step) % n_images, 1, 0)
            for step in range(n_images)
        ]
    )
    turned_final = (turned_gates.T[:, :, None] * w_final.astype(F32)[:, None, :]).astype(BF16)
    turned_final = turned_final.reshape(width_d, n_images * lat)
    out_strip = matmul(turned_final, inner).astype(BF16)
    out_strip, terms = lax.optimization_barrier((out_strip, terms))
    out_strips = exchanged(out_strip.reshape(n_rows, d_dev, strip), ROWS_AT)
    grad_out_t = jnp.moveaxis(out_strips, 0, 1).reshape(d_dev, ff_mp).astype(F32)

    grad_in = jnp.sum(terms.reshape(n_near, n_images, d_dev, half).astype(F32), axis=1)
    grad_in = jnp.moveaxis(grad_in, 0, 1).reshape(d_dev, ff_mp)
    return (grad_in, grad_out_t)


def solution(mesh):
    n_group, n_dp, n_mp = (mesh.shape[axis] for axis in ("group", "dp", "mp"))
    fine = Mesh(mesh.devices.reshape(n_group, n_dp // 2, 2, n_mp // 2, 2), AXES)
    tokens = ("y", "core")
    weights = P(ROWS_AT, tokens)
    placed = (
        P(IMAGE, tokens, None),
        P(IMAGE),
        P(),
        P(IMAGE, tokens, None),
        P(),
        weights,
        weights,
        P(),
        P(),
        P(),
        P(),
        P(None, tokens),
        P(tokens, None),
    )
    return jax.shard_map(
        on_device, mesh=fine, in_specs=placed, out_specs=(weights, weights), check_vma=False
    )
```

```python
import math

import jax
import jax.numpy as jnp
from jax import lax
from jax.experimental import pallas as pl
from jax.experimental.pallas import tpu as pltpu
from jax.sharding import Mesh
from jax.sharding import PartitionSpec as P

BF16 = jnp.bfloat16
GELU_SCALE = math.sqrt(2.0 / math.pi)
VMEM_BYTES = 24 * 1024 * 1024
F32 = jnp.float32
AXES = ("near", "z", "far", "y", "core")
IMAGE = ("z", "far")
ROWS_AT = ("near", "z", "far")
FAR_FIRST = ("far", "near", "z")
PAIR_ROWS = ("near", "z")
TOKENS_AT = ("near", "y", "core")


def layer_norm(values):
    mean = jnp.mean(values, axis=-1, keepdims=True)
    centred = values - mean
    variance = jnp.mean(centred * centred, axis=-1, keepdims=True)
    return centred * lax.rsqrt(variance + 1e-06)


def gelu_and_slope(values):
    inner = GELU_SCALE * (values + 0.044715 * values * values * values)
    bent = jnp.tanh(inner)
    half = 0.5 * (1.0 + bent)
    rate = GELU_SCALE * (1.0 + 3 * 0.044715 * values * values)
    return values * half, half + 0.5 * values * (1.0 - bent * bent) * rate


def silu_and_slope(values):
    gate = jax.nn.sigmoid(values)
    result = values * gate
    return result, gate + result * (1.0 - gate)


def norm_back(values, cotangent):
    _, pullback = jax.vjp(layer_norm, values)
    return pullback(cotangent)[0]


def matmul(left, right):
    return jnp.dot(left, right, preferred_element_type=F32)


def matmul_nt(left, right):
    return lax.dot_general(left, right, (((1,), (1,)), ((), ())), preferred_element_type=F32)


def matmul_tn(left, right):
    return lax.dot_general(left, right, (((0,), (0,)), ((), ())), preferred_element_type=F32)


def turned(value, axis, steps):
    count = lax.axis_size(axis)
    return lax.ppermute(value, axis, [(at, (at + steps) % count) for at in range(count)])


def from_all(value, axis):
    count = lax.axis_size(axis)
    return [value] + [turned(value, axis, step) for step in range(1, count)]


def summed_back(blocks, axis):
    total = blocks[0].astype(F32)
    for step in range(1, len(blocks)):
        total = total + turned(blocks[step], axis, -step).astype(F32)
    return total


def exchanged(blocks, axis):
    return lax.all_to_all(blocks, axis, 0, 0, tiled=True)


def whole(array):
    return pl.BlockSpec(array.shape, lambda step: (0,) * len(array.shape))


def call(kernel, grid, in_specs, out_specs, out_shape, scratch, flops, moved, *operands):
    return pl.pallas_call(
        kernel,
        grid=(grid,),
        in_specs=in_specs,
        out_specs=out_specs,
        out_shape=out_shape,
        scratch_shapes=scratch,
        compiler_params=pltpu.CompilerParams(vmem_limit_bytes=VMEM_BYTES),
        cost_estimate=pl.CostEstimate(flops=flops, bytes_accessed=moved, transcendentals=0),
    )(*operands)


def block_forward_kernel(tokens, weights, hidden, slope):
    total = matmul(tokens[0], weights[0]) + matmul(tokens[1], weights[1])
    act, rate = gelu_and_slope(total)
    hidden[...] = act.astype(BF16)
    slope[...] = rate.astype(BF16)


def block_forward(tokens, weights):
    parts, rows, width = tokens.shape
    columns = weights.shape[2]
    tile = rows // 4
    return call(
        block_forward_kernel,
        4,
        [pl.BlockSpec((parts, tile, width), lambda step: (0, step, 0)), whole(weights)],
        [pl.BlockSpec((tile, columns), lambda step: (step, 0))] * 2,
        [jax.ShapeDtypeStruct((rows, columns), BF16)] * 2,
        [],
        2 * rows * columns * parts * width,
        2 * (parts * rows * width + parts * width * columns + 2 * rows * columns),
        tokens,
        weights,
    )


def block_backward_kernel(grads, through, slope, tokens, grads2, through2, slope2, tokens2, term, pre, pre2):
    @pl.when(pl.program_id(0) == 0)
    def _():
        back = matmul_nt(grads[...], through[...])
        pre[...] = (slope[...].astype(F32) * back).astype(BF16)
        back = matmul_nt(grads2[...], through2[...])
        pre2[...] = (slope2[...].astype(F32) * back).astype(BF16)

    total = matmul_tn(tokens[...], pre[...]) + matmul_tn(tokens2[...], pre2[...])
    term[...] = total.astype(BF16)


def block_backward(images):
    rows, width = images[0][3].shape
    columns = images[0][2].shape[1]
    tile = min(640, width)
    cut = pl.BlockSpec((rows, tile), lambda step: (0, step))
    specs = []
    for grads, through, slope, _ in images:
        specs += [whole(grads), whole(through), whole(slope), cut]
    return call(
        block_backward_kernel,
        pl.cdiv(width, tile),
        specs,
        pl.BlockSpec((tile, columns), lambda step: (step, 0)),
        jax.ShapeDtypeStruct((width, columns), BF16),
        [pltpu.VMEM((rows, columns), BF16)] * 2,
        4 * rows * columns * width,
        2 * (2 * rows * width + width * columns + 2 * rows * columns),
        *images[0],
        *images[1],
    )


def decode_kernel(latent, w_dec1, w_dec2, w_patch, normed, embedded, slope, pixels):
    step = pl.program_id(0)
    act, rate = silu_and_slope(matmul(latent[...], w_dec1[...]))
    slope[...] = rate[: slope.shape[0]]
    part = matmul(act.astype(BF16), w_dec2[...])

    @pl.when(step == 0)
    def _():
        pixels[...] = part

    @pl.when(step > 0)
    def _():
        pixels[...] += part

    @pl.when(step == pl.num_programs(0) - 1)
    def _():
        patches = matmul(pixels[...].astype(BF16), w_patch[...])
        normed[...] = layer_norm(patches).astype(BF16)
        embedded[...] = patches[: embedded.shape[0]]


def decode(latent, w_dec1, w_dec2, w_patch, mine):
    rows, lat = latent.shape
    deep, pix = w_dec2.shape
    width = w_patch.shape[1]
    tile = min(512, deep)
    return call(
        decode_kernel,
        deep // tile,
        [
            whole(latent),
            pl.BlockSpec((lat, tile), lambda step: (0, step)),
            pl.BlockSpec((tile, pix), lambda step: (step, 0)),
            whole(w_patch),
        ],
        [
            pl.BlockSpec((rows, width), lambda step: (0, 0)),
            pl.BlockSpec((mine, width), lambda step: (0, 0)),
            pl.BlockSpec((mine, tile), lambda step: (0, step)),
        ],
        [
            jax.ShapeDtypeStruct((rows, width), BF16),
            jax.ShapeDtypeStruct((mine, width), F32),
            jax.ShapeDtypeStruct((mine, deep), F32),
        ],
        [pltpu.VMEM((rows, pix), F32)],
        2 * rows * (lat * deep + deep * pix + pix * width),
        2 * (deep * pix + pix * width),
        latent,
        w_dec1,
        w_dec2,
        w_patch,
    )


def reward_forward_kernel(normed, v1a, v1b, v2a, v2b, slope_a, slope_b, out, total):
    step = pl.program_id(0)
    part = 0.0
    for v1, v2, slope in ((v1a, v2a, slope_a), (v1b, v2b, slope_b)):
        act, rate = gelu_and_slope(matmul(normed[...], v1[...]))
        slope[...] = rate
        part = part + matmul(act.astype(BF16), v2[...])

    @pl.when(step == 0)
    def _():
        total[...] = part

    @pl.when(step > 0)
    def _():
        total[...] += part

    @pl.when(step == pl.num_programs(0) - 1)
    def _():
        out[...] = total[...].astype(BF16)


def reward_backward_kernel(grad, v1a, v1b, v2a, v2b, slope_a, slope_b, out, total):
    step = pl.program_id(0)
    part = 0.0
    for v1, v2, slope in ((v1a, v2a, slope_a), (v1b, v2b, slope_b)):
        back = (slope[...] * matmul_nt(grad[...], v2[...])).astype(BF16)
        part = part + matmul_nt(back, v1[...])

    @pl.when(step == 0)
    def _():
        total[...] = part

    @pl.when(step > 0)
    def _():
        total[...] += part

    @pl.when(step == pl.num_programs(0) - 1)
    def _():
        out[...] = total[...].astype(BF16)


def reward(values, v1_both, v2_both, slopes=None):
    rows, width = values.shape
    hidden = v1_both[0].shape[1]
    tile = min(128, hidden)
    slope_spec = pl.BlockSpec((rows, tile), lambda step: (0, step))
    slope_shape = jax.ShapeDtypeStruct((rows, hidden), F32)
    out_spec = pl.BlockSpec((rows, width), lambda step: (0, 0))
    out_shape = jax.ShapeDtypeStruct((rows, width), BF16)
    v1_spec = pl.BlockSpec((width, tile), lambda step: (0, step))
    v2_spec = pl.BlockSpec((tile, width), lambda step: (step, 0))
    weight_specs = [whole(values), v1_spec, v1_spec, v2_spec, v2_spec]
    forward = slopes is None
    return call(
        reward_forward_kernel if forward else reward_backward_kernel,
        hidden // tile,
        weight_specs + ([] if forward else [slope_spec] * 2),
        [slope_spec] * 2 + [out_spec] if forward else out_spec,
        [slope_shape] * 2 + [out_shape] if forward else out_shape,
        [pltpu.VMEM((rows, width), F32)],
        8 * rows * width * hidden,
        8 * width * hidden,
        values,
        *v1_both,
        *v2_both,
        *(() if forward else slopes),
    )


def on_device(
    latent_noise,
    timestep,
    reward_slot,
    target,
    modulation,
    w_in,
    w_out_t,
    w_final,
    w_dec1,
    w_dec2,
    w_patch,
    w_v1,
    w_v2,
):
    tok_dev = latent_noise.shape[1]
    n_near, n_y, n_core = (lax.axis_size(axis) for axis in TOKENS_AT)
    n_images = lax.axis_size("z") * lax.axis_size("far")
    n_rows = n_near * n_images
    n_tokens = n_near * n_y * n_core
    mine = tok_dev // n_near
    rows = tok_dev * n_y * n_core
    d_dev, ff_mp = w_in.shape
    width_d = d_dev * n_rows
    half = ff_mp // n_near
    strip = ff_mp // n_rows
    lat = w_final.shape[1]
    scale = 1.0 / math.sqrt(n_images * rows)
    near = lax.axis_index("near")
    my_image = lax.axis_index(IMAGE)
    my_slot = reward_slot[my_image]

    n_z, n_far = lax.axis_size("z"), lax.axis_size("far")
    far = lax.axis_index("far")
    wide = width_d // n_far

    split_in = jnp.moveaxis(w_in.reshape(d_dev, n_near, half), 1, 0)
    split_in = jnp.broadcast_to(split_in[None, :, None], (n_far, n_near, n_z, d_dev, half))
    split_in = split_in.reshape(n_rows, d_dev, half)
    split_in, noise_rows = lax.optimization_barrier((split_in, latent_noise[0]))
    full_in = exchanged(split_in, FAR_FIRST).reshape(n_far, wide, half)

    modulate = modulation[timestep[0]]
    modulated = (
        layer_norm(noise_rows.astype(F32)) * (1.0 + modulate[1]) + modulate[0]
    ).astype(BF16)
    modulated = modulated.reshape(tok_dev, n_rows // n_far, n_far, d_dev)
    modulated = jnp.moveaxis(modulated, 2, 0).reshape(n_far, tok_dev, wide)
    token_rows = lax.all_gather(modulated, ("y", "core"), axis=1, tiled=True)

    strips = jnp.moveaxis(w_out_t.reshape(d_dev, n_rows, strip), 1, 0)
    steps_row = jnp.broadcast_to(timestep[0].astype(BF16), (n_rows, 8, strip))
    strips = jnp.concatenate([strips, steps_row], axis=1)
    strips, full_in = lax.optimization_barrier((strips, full_in))
    arrived = exchanged(strips, ROWS_AT)
    strip_rows = arrived[:, :d_dev].reshape(width_d, strip)
    all_steps = arrived[:n_images, d_dev, 0].astype(jnp.int32)
    gates = modulation[all_steps, 2]
    gated_final = (gates.T[:, :, None] * w_final.astype(F32)[:, None, :]).astype(BF16)
    through = matmul_tn(strip_rows, gated_final.reshape(width_d, n_images * lat)).astype(BF16)
    through = exchanged(jnp.moveaxis(through.reshape(strip, n_images, lat), 1, 0), IMAGE)
    through = through.reshape(half, lat)

    v1_both = (w_v1, turned(w_v1, "core", 1))
    v2_both = (w_v2, turned(w_v2, "core", 1))

    hidden, hidden_slope = block_forward(token_rows, full_in)
    own_target, hidden = lax.optimization_barrier((target[0], hidden))
    goals = lax.all_gather(own_target, IMAGE, axis=0)
    goal = lax.dynamic_slice(goals, (my_slot, near * mine, 0), (1, mine, goals.shape[2]))[0]
    goal = goal.astype(F32)
    kept_rows = lax.dynamic_index_in_dim(token_rows, far, 0, keepdims=False)
    far_rows = lax.dynamic_index_in_dim(token_rows, 1 - far, 0, keepdims=False)
    far_rows, hidden_slope = lax.optimization_barrier((far_rows, hidden_slope))
    far_rows = turned(far_rows, "far", 1)
    far_slope = turned(hidden_slope, "far", 1)
    far_through = turned(through, "far", 1)
    n_mp = n_y * n_core
    own_part = matmul(noise_rows, w_final).reshape(1, n_near, mine, lat)
    here = (lax.iota(jnp.int32, n_mp) == lax.axis_index(("y", "core")))[:, None]
    here = here & (lax.iota(jnp.int32, n_near) == near)[None]
    latent_part = matmul(hidden, through).reshape(n_mp, n_near, mine, lat)
    latent_part = (latent_part + jnp.where(here[:, :, None, None], own_part, 0.0)).astype(BF16)
    latent_part = latent_part.reshape(n_y, n_core, n_near, mine, lat).transpose(2, 1, 0, 3, 4)
    latent_part = jnp.broadcast_to(latent_part[:, None], (n_near, n_y) + latent_part.shape[1:])
    latent_parts = exchanged(latent_part.reshape(n_tokens, n_y * mine, lat), TOKENS_AT)
    latents = jnp.sum(latent_parts.astype(F32), axis=0).astype(BF16)
    my_y = lax.axis_index("y")
    latent = jnp.concatenate(
        [
            lax.dynamic_slice_in_dim(latents, (my_y - step) % n_y * mine, mine, 0)
            for step in range(n_y)
        ]
    )

    patch_rows, embedded, dec_slope = decode(latent, w_dec1, w_dec2, w_patch, mine)
    *slopes, vit_part = reward(patch_rows, v1_both, v2_both)
    vit_out = summed_back(jnp.split(vit_part, n_y), "y")
    feature_grad = ((embedded + vit_out - goal) * scale).astype(BF16)

    grad_rows = jnp.concatenate(from_all(feature_grad, "y"))
    norm_part = reward(grad_rows, v1_both, v2_both, slopes)
    norm_grad = summed_back(jnp.split(norm_part, n_y), "y")
    embed_grad = (feature_grad.astype(F32) + norm_back(embedded, norm_grad)).astype(BF16)
    pixel_grad = matmul_nt(embed_grad, w_patch).astype(BF16)
    dec_pre_grad = (dec_slope * matmul_nt(pixel_grad, w_dec2)).astype(BF16)
    latent_grad = matmul_nt(dec_pre_grad, w_dec1).astype(BF16)

    spread = jnp.broadcast_to(latent_grad, (n_far * n_tokens, mine, lat))
    spread = exchanged(spread, ("far",) + TOKENS_AT)
    spread = spread.reshape(n_far, n_near, n_y * n_core, mine, lat)
    spread = jnp.moveaxis(spread, 1, 2).reshape(n_far, rows, lat)
    latent_rows = lax.dynamic_index_in_dim(spread, far, 0, keepdims=False)
    far_latent_rows = lax.dynamic_index_in_dim(spread, 1 - far, 0, keepdims=False)

    inner = matmul_tn(latent_rows, hidden).astype(BF16)
    far_inner = turned(inner, "far", 1)
    term_in = block_backward(
        (
            (latent_rows, through, hidden_slope, kept_rows),
            (far_latent_rows, far_through, far_slope, far_rows),
        )
    )
    both = jnp.concatenate([inner, far_inner])
    both = jnp.broadcast_to(both, (n_near * n_z,) + both.shape)
    sent = jnp.concatenate([term_in.reshape(n_near * n_z, d_dev, half), both], axis=1)
    came = exchanged(sent, PAIR_ROWS).reshape(n_near, n_z, d_dev + 2 * lat, half)
    grad_in = jnp.sum(came[:, :, :d_dev].astype(F32), axis=1)
    grad_in = jnp.moveaxis(grad_in, 0, 1).reshape(d_dev, ff_mp)

    at = lax.axis_index(ROWS_AT) * d_dev
    my_final = lax.dynamic_slice_in_dim(w_final, at, d_dev, 0).astype(F32)
    my_gates = lax.dynamic_slice_in_dim(gates, at, d_dev, 1).reshape(n_z, n_far, d_dev)
    my_gates = jnp.where(far == 0, my_gates, my_gates[:, ::-1])
    my_gated = my_gates.reshape(n_images, d_dev).T[:, :, None] * my_final[:, None, :]
    my_gated = my_gated.astype(BF16).reshape(d_dev, n_images * lat)
    outs = [
        matmul(my_gated, came[at_near, :, d_dev:].reshape(n_images * lat, half))
        for at_near in range(n_near)
    ]
    return (grad_in, jnp.concatenate(outs, axis=1))


def solution(mesh):
    n_group, n_dp, n_mp = (mesh.shape[axis] for axis in ("group", "dp", "mp"))
    fine = Mesh(mesh.devices.reshape(n_group, n_dp // 2, 2, n_mp // 2, 2), AXES)
    tokens = ("y", "core")
    weights = P(ROWS_AT, tokens)
    placed = (
        P(IMAGE, tokens, None),
        P(IMAGE),
        P(),
        P(IMAGE, tokens, None),
        P(),
        weights,
        weights,
        P(),
        P(),
        P(),
        P(),
        P(None, tokens),
        P(tokens, None),
    )
    return jax.shard_map(
        on_device, mesh=fine, in_specs=placed, out_specs=(weights, weights), check_vma=False
    )
```

```python
import math

import jax
import jax.numpy as jnp
from jax import lax
from jax.experimental import pallas as pl
from jax.experimental.pallas import tpu as pltpu
from jax.sharding import Mesh
from jax.sharding import PartitionSpec as P

BF16 = jnp.bfloat16
GELU_SCALE = math.sqrt(2.0 / math.pi)
MIB = 1024 * 1024
SMALL, LARGE = 24 * MIB, 56 * MIB
F32 = jnp.float32
AXES = ("near", "z", "far", "y", "core")
IMAGE = ("z", "far")
ROWS_AT = ("near", "z", "far")
FAR_FIRST = ("far", "near", "z")
PAIR_ROWS = ("near", "z")
TOKENS_AT = ("near", "y", "core")


def layer_norm(values):
    mean = jnp.mean(values, axis=-1, keepdims=True)
    centred = values - mean
    variance = jnp.mean(centred * centred, axis=-1, keepdims=True)
    return centred * lax.rsqrt(variance + 1e-06)


def gelu_and_slope(values):
    inner = GELU_SCALE * (values + 0.044715 * values * values * values)
    bent = jnp.tanh(inner)
    half = 0.5 * (1.0 + bent)
    rate = GELU_SCALE * (1.0 + 3 * 0.044715 * values * values)
    return values * half, half + 0.5 * values * (1.0 - bent * bent) * rate


def silu_and_slope(values):
    gate = jax.nn.sigmoid(values)
    result = values * gate
    return result, gate + result * (1.0 - gate)


def norm_back(values, cotangent):
    _, pullback = jax.vjp(layer_norm, values)
    return pullback(cotangent)[0]


def matmul(left, right):
    return jnp.dot(left, right, preferred_element_type=F32)


def matmul_nt(left, right):
    return lax.dot_general(left, right, (((1,), (1,)), ((), ())), preferred_element_type=F32)


def matmul_tn(left, right):
    return lax.dot_general(left, right, (((0,), (0,)), ((), ())), preferred_element_type=F32)


def turned(value, axis, steps):
    count = lax.axis_size(axis)
    return lax.ppermute(value, axis, [(at, (at + steps) % count) for at in range(count)])


def from_all(value, axis):
    count = lax.axis_size(axis)
    return [value] + [turned(value, axis, step) for step in range(1, count)]


def summed_back(blocks, axis):
    total = blocks[0].astype(F32)
    for step in range(1, len(blocks)):
        total = total + turned(blocks[step], axis, -step).astype(F32)
    return total


def exchanged(blocks, axis):
    return lax.all_to_all(blocks, axis, 0, 0, tiled=True)


def lanes(columns):
    return pl.cdiv(columns, 128) * 128


def whole(array):
    return pl.BlockSpec(array.shape, lambda step: (0,) * len(array.shape))


SCALARS = pl.BlockSpec(memory_space=pltpu.SMEM)


def call(kernel, grid, in_specs, out_specs, out_shape, scratch, flops, moved, limit, *operands):
    return pl.pallas_call(
        kernel,
        grid=(grid,),
        in_specs=in_specs,
        out_specs=out_specs,
        out_shape=out_shape,
        scratch_shapes=scratch,
        compiler_params=pltpu.CompilerParams(vmem_limit_bytes=limit),
        cost_estimate=pl.CostEstimate(flops=flops, bytes_accessed=moved, transcendentals=0),
    )(*operands)


def block_forward_kernel(at, tokens, weights, hidden, slope):
    far = at[0]
    total = matmul(tokens[0], weights[far]) + matmul(tokens[1], weights[1 - far])
    act, rate = gelu_and_slope(total)
    columns = act.shape[1]
    hidden[...] = act.astype(BF16)
    slope[:, :columns] = rate.astype(BF16)
    if slope.shape[1] > columns:
        slope[:, columns:] = jnp.zeros((act.shape[0], slope.shape[1] - columns), BF16)


def block_forward(at, tokens, weights):
    parts, rows, width = tokens.shape
    columns = weights.shape[2]
    tile = rows // 4
    return call(
        block_forward_kernel,
        4,
        [
            SCALARS,
            pl.BlockSpec((parts, tile, width), lambda step: (0, step, 0)),
            whole(weights),
        ],
        [
            pl.BlockSpec((tile, columns), lambda step: (step, 0)),
            pl.BlockSpec((tile, lanes(columns)), lambda step: (step, 0)),
        ],
        [
            jax.ShapeDtypeStruct((rows, columns), BF16),
            jax.ShapeDtypeStruct((rows, lanes(columns)), BF16),
        ],
        [],
        2 * rows * columns * parts * width,
        2 * (parts * rows * width + parts * width * columns + 2 * rows * columns),
        LARGE,
        at,
        tokens,
        weights,
    )


def latent_kernel(at, hidden, through, own_part, out, total):
    n_near, n_y, n_core, _, mine, _ = out.shape
    lat = through.shape[1]
    near, place = at[1], at[2]
    total[...] = matmul(hidden[...], through[...])
    rows = pl.ds(pl.multiple_of((place * n_near + near) * mine, mine), mine)
    total[rows] += own_part[pl.ds(pl.multiple_of(near * mine, mine), mine)]
    for y in range(n_y):
        for core in range(n_core):
            for side in range(n_near):
                start = ((y * n_core + core) * n_near + side) * mine
                block = total[start : start + mine].astype(BF16)
                for other in range(n_y):
                    out[side, other, core, y // 2, :, y % 2 * lat : (y % 2 + 1) * lat] = block


def latent_parts_of(at, hidden, through, own_part, shape):
    rows, columns = hidden.shape
    lat = through.shape[1]
    return call(
        latent_kernel,
        1,
        [SCALARS, whole(hidden), whole(through), whole(own_part)],
        pl.BlockSpec(shape, lambda step: (0,) * len(shape)),
        jax.ShapeDtypeStruct(shape, BF16),
        [pltpu.VMEM((rows, lat), F32)],
        2 * rows * columns * lat,
        2 * rows * columns,
        SMALL,
        at,
        hidden,
        through,
        own_part,
    )


def inner_kernel(at, spread, hidden, grads, far_grads, inner):
    _, n_near, n_mp, mine, _ = spread.shape
    for image, result in ((at[0], grads), (1 - at[0], far_grads)):
        for place in range(n_mp):
            for near in range(n_near):
                start = (place * n_near + near) * mine
                result[start : start + mine] = spread[image, near, place]
    inner[...] = matmul_tn(grads[:, : inner.shape[0]], hidden[...]).astype(BF16)


def inner_products(at, spread, hidden, lat):
    rows, columns = hidden.shape
    shapes = [
        jax.ShapeDtypeStruct((rows, spread.shape[-1]), BF16),
        jax.ShapeDtypeStruct((rows, spread.shape[-1]), BF16),
        jax.ShapeDtypeStruct((lat, columns), BF16),
    ]
    return call(
        inner_kernel,
        1,
        [SCALARS, whole(spread), whole(hidden)],
        [whole(shape) for shape in shapes],
        shapes,
        [],
        2 * rows * columns * lat,
        2 * rows * columns,
        SMALL,
        at,
        spread,
        hidden,
    )


def block_backward_kernel(
    grads, through, slope, tokens, grads2, through2, slope2, tokens2, term, pre, pre2
):
    @pl.when(pl.program_id(0) == 0)
    def _():
        columns, lat = through.shape
        for grad, via, rate, result in (
            (grads, through, slope, pre),
            (grads2, through2, slope2, pre2),
        ):
            back = matmul_nt(grad[:, :lat], via[...])
            result[...] = (rate[:, :columns].astype(F32) * back).astype(BF16)

    total = matmul_tn(tokens[0], pre[...]) + matmul_tn(tokens2[...], pre2[...])
    term[...] = total.astype(BF16)


def block_backward(grads, through, slope, tokens, grads2, through2, slope2, tokens2):
    rows, width = tokens2.shape
    columns = through.shape[0]
    tile = min(640, width)
    return call(
        block_backward_kernel,
        pl.cdiv(width, tile),
        [
            whole(grads),
            whole(through),
            whole(slope),
            pl.BlockSpec((1, rows, tile), lambda step: (0, 0, step)),
            whole(grads2),
            whole(through2),
            whole(slope2),
            pl.BlockSpec((rows, tile), lambda step: (0, step)),
        ],
        pl.BlockSpec((tile, columns), lambda step: (step, 0)),
        jax.ShapeDtypeStruct((width, columns), BF16),
        [pltpu.VMEM((rows, columns), BF16)] * 2,
        4 * rows * columns * width,
        2 * (2 * rows * width + width * columns + 2 * rows * columns),
        LARGE,
        grads,
        through,
        slope,
        tokens,
        grads2,
        through2,
        slope2,
        tokens2,
    )


def decode_kernel(at, parts, w_dec1, w_dec2, w_patch, normed, embedded, slope, pixels, total, latent):
    step = pl.program_id(0)

    @pl.when(step == 0)
    def _():
        n_parts, pairs, mine, _ = parts.shape
        count = total.shape[0]
        lat = total.shape[2]
        added = parts[0].astype(F32)
        for source in range(1, n_parts):
            added = added + parts[source].astype(F32)
        for pair in range(pairs):
            total[2 * pair] = added[pair, :, :lat]
            total[2 * pair + 1] = added[pair, :, lat:]
        for turn in range(count):
            owner = lax.rem(at[3] - turn + count, count)
            latent[turn * mine : (turn + 1) * mine] = total[owner].astype(BF16)

    act, rate = silu_and_slope(matmul(latent[...], w_dec1[...]))
    slope[...] = rate[: slope.shape[0]]
    part = matmul(act.astype(BF16), w_dec2[...])

    @pl.when(step == 0)
    def _():
        pixels[...] = part

    @pl.when(step > 0)
    def _():
        pixels[...] += part

    @pl.when(step == pl.num_programs(0) - 1)
    def _():
        patches = matmul(pixels[...].astype(BF16), w_patch[...])
        normed[...] = layer_norm(patches).astype(BF16)
        embedded[...] = patches[: embedded.shape[0]]


def decode(at, parts, w_dec1, w_dec2, w_patch, mine):
    count, lat = 2 * parts.shape[1], parts.shape[3] // 2
    rows = count * mine
    deep, pix = w_dec2.shape
    width = w_patch.shape[1]
    tile = min(512, deep)
    return call(
        decode_kernel,
        deep // tile,
        [
            SCALARS,
            whole(parts),
            pl.BlockSpec((lat, tile), lambda step: (0, step)),
            pl.BlockSpec((tile, pix), lambda step: (step, 0)),
            whole(w_patch),
        ],
        [
            pl.BlockSpec((rows, width), lambda step: (0, 0)),
            pl.BlockSpec((mine, width), lambda step: (0, 0)),
            pl.BlockSpec((mine, tile), lambda step: (0, step)),
        ],
        [
            jax.ShapeDtypeStruct((rows, width), BF16),
            jax.ShapeDtypeStruct((mine, width), F32),
            jax.ShapeDtypeStruct((mine, deep), F32),
        ],
        [
            pltpu.VMEM((rows, pix), F32),
            pltpu.VMEM((count, mine, lat), F32),
            pltpu.VMEM((rows, lat), BF16),
        ],
        2 * rows * (lat * deep + deep * pix + pix * width),
        2 * (deep * pix + pix * width),
        SMALL,
        at,
        parts,
        w_dec1,
        w_dec2,
        w_patch,
    )


def reward_forward_kernel(normed, v1a, v1b, v2a, v2b, slope_a, slope_b, out, total):
    step = pl.program_id(0)
    part = 0.0
    for v1, v2, slope in ((v1a, v2a, slope_a), (v1b, v2b, slope_b)):
        act, rate = gelu_and_slope(matmul(normed[...], v1[...]))
        slope[...] = rate
        part = part + matmul(act.astype(BF16), v2[...])

    @pl.when(step == 0)
    def _():
        total[...] = part

    @pl.when(step > 0)
    def _():
        total[...] += part

    @pl.when(step == pl.num_programs(0) - 1)
    def _():
        out[...] = total[...].astype(BF16)


def reward_backward_kernel(grad, v1a, v1b, v2a, v2b, slope_a, slope_b, out, total):
    step = pl.program_id(0)
    part = 0.0
    for v1, v2, slope in ((v1a, v2a, slope_a), (v1b, v2b, slope_b)):
        back = (slope[...] * matmul_nt(grad[...], v2[...])).astype(BF16)
        part = part + matmul_nt(back, v1[...])

    @pl.when(step == 0)
    def _():
        total[...] = part

    @pl.when(step > 0)
    def _():
        total[...] += part

    @pl.when(step == pl.num_programs(0) - 1)
    def _():
        out[...] = total[...].astype(BF16)


def reward(values, v1_both, v2_both, slopes=None):
    rows, width = values.shape
    hidden = v1_both[0].shape[1]
    tile = hidden
    slope_spec = pl.BlockSpec((rows, tile), lambda step: (0, step))
    slope_shape = jax.ShapeDtypeStruct((rows, hidden), F32)
    out_spec = pl.BlockSpec((rows, width), lambda step: (0, 0))
    out_shape = jax.ShapeDtypeStruct((rows, width), BF16)
    v1_spec = pl.BlockSpec((width, tile), lambda step: (0, step))
    v2_spec = pl.BlockSpec((tile, width), lambda step: (step, 0))
    weight_specs = [whole(values), v1_spec, v1_spec, v2_spec, v2_spec]
    forward = slopes is None
    return call(
        reward_forward_kernel if forward else reward_backward_kernel,
        hidden // tile,
        weight_specs + ([] if forward else [slope_spec] * 2),
        [slope_spec] * 2 + [out_spec] if forward else out_spec,
        [slope_shape] * 2 + [out_shape] if forward else out_shape,
        [pltpu.VMEM((rows, width), F32)],
        8 * rows * width * hidden,
        8 * width * hidden,
        SMALL,
        values,
        *v1_both,
        *v2_both,
        *(() if forward else slopes),
    )


def on_device(
    latent_noise,
    timestep,
    reward_slot,
    target,
    modulation,
    w_in,
    w_out_t,
    w_final,
    w_dec1,
    w_dec2,
    w_patch,
    w_v1,
    w_v2,
):
    tok_dev = latent_noise.shape[1]
    n_near, n_y, n_core = (lax.axis_size(axis) for axis in TOKENS_AT)
    n_images = lax.axis_size("z") * lax.axis_size("far")
    n_rows = n_near * n_images
    n_tokens = n_near * n_y * n_core
    mine = tok_dev // n_near
    rows = tok_dev * n_y * n_core
    d_dev, ff_mp = w_in.shape
    width_d = d_dev * n_rows
    half = ff_mp // n_near
    strip = ff_mp // n_rows
    lat = w_final.shape[1]
    scale = 1.0 / math.sqrt(n_images * rows)
    near = lax.axis_index("near")
    my_image = lax.axis_index(IMAGE)
    my_slot = reward_slot[my_image]

    n_z, n_far = lax.axis_size("z"), lax.axis_size("far")
    far = lax.axis_index("far")
    wide = width_d // n_far

    at = jnp.stack([far, near, lax.axis_index(("y", "core")), lax.axis_index("y")]).astype(jnp.int32)

    strips = jnp.moveaxis(w_out_t.reshape(d_dev, n_rows, strip), 1, 0)
    steps_row = jnp.broadcast_to(timestep[0].astype(BF16), (n_rows, 8, strip))
    strips = jnp.concatenate([strips, steps_row], axis=1)
    strips, w_in, noise_rows = lax.optimization_barrier((strips, w_in, latent_noise[0]))
    arrived = exchanged(strips, ROWS_AT)

    split_in = jnp.moveaxis(w_in.reshape(d_dev, n_near, half), 1, 0)
    split_in = jnp.broadcast_to(split_in[None, :, None], (n_far, n_near, n_z, d_dev, half))
    split_in = split_in.reshape(n_rows, d_dev, half)

    modulate = modulation[timestep[0]]
    modulated = (
        layer_norm(noise_rows.astype(F32)) * (1.0 + modulate[1]) + modulate[0]
    ).astype(BF16)
    modulated = modulated.reshape(tok_dev, n_rows // n_far, n_far, d_dev)
    modulated = jnp.moveaxis(modulated, 2, 0).reshape(n_far, tok_dev, wide)
    modulated = jnp.where(far == 0, modulated, modulated[::-1])
    modulated, split_in = lax.optimization_barrier((modulated, split_in))
    token_rows = lax.all_gather(modulated, ("y", "core"), axis=1, tiled=True)
    far_rows = lax.all_gather(turned(modulated[1], "far", 1), ("y", "core"), axis=0, tiled=True)

    arrived, split_in = lax.optimization_barrier((arrived, split_in))
    full_in = exchanged(split_in, FAR_FIRST).reshape(n_far, wide, half)

    strip_rows = arrived[:, :d_dev].reshape(width_d, strip)
    all_steps = arrived[:n_images, d_dev, 0].astype(jnp.int32)
    gates = modulation[all_steps, 2]
    gated_final = (gates.T[:, :, None] * w_final.astype(F32)[:, None, :]).astype(BF16)
    through = matmul_tn(strip_rows, gated_final.reshape(width_d, n_images * lat)).astype(BF16)
    through = jnp.moveaxis(through.reshape(strip, n_images, lat), 1, 0)
    through, full_in, own_target = lax.optimization_barrier((through, full_in, target[0]))
    through = exchanged(through, IMAGE).reshape(half, lat)

    v1_both = (w_v1, turned(w_v1, "core", 1))
    v2_both = (w_v2, turned(w_v2, "core", 1))

    hidden, hidden_slope = block_forward(at, token_rows, full_in)
    goals = lax.all_gather(own_target, IMAGE, axis=0)
    goal = lax.dynamic_slice(goals, (my_slot, near * mine, 0), (1, mine, goals.shape[2]))[0]
    goal = goal.astype(F32)
    far_slope = turned(hidden_slope, "far", 1)
    far_through = turned(through, "far", 1)
    own_part = matmul(noise_rows, w_final)
    shape = (n_near, n_y, n_core, n_y // 2, mine, 2 * lat)
    latent_part = latent_parts_of(at, hidden, through, own_part, shape)
    latent_parts = exchanged(latent_part.reshape(n_tokens, n_y // 2, mine, 2 * lat), TOKENS_AT)

    patch_rows, embedded, dec_slope = decode(at, latent_parts, w_dec1, w_dec2, w_patch, mine)
    *slopes, vit_part = reward(patch_rows, v1_both, v2_both)
    vit_out = summed_back(jnp.split(vit_part, n_y), "y")
    feature_grad = ((embedded + vit_out - goal) * scale).astype(BF16)
    feature_grad, far_slope, far_through = lax.optimization_barrier(
        (feature_grad, far_slope, far_through)
    )

    grad_rows = jnp.concatenate(from_all(feature_grad, "y"))
    norm_part = reward(grad_rows, v1_both, v2_both, slopes)
    norm_grad = summed_back(jnp.split(norm_part, n_y), "y")
    embed_grad = (feature_grad.astype(F32) + norm_back(embedded, norm_grad)).astype(BF16)
    pixel_grad = matmul_nt(embed_grad, w_patch).astype(BF16)
    dec_pre_grad = (dec_slope * matmul_nt(pixel_grad, w_dec2)).astype(BF16)
    latent_grad = matmul_nt(dec_pre_grad, w_dec1).astype(BF16)

    latent_grad = jnp.pad(latent_grad, ((0, 0), (0, lanes(lat) - lat)))
    spread = jnp.broadcast_to(latent_grad, (n_far * n_tokens,) + latent_grad.shape)
    spread = exchanged(spread, ("far",) + TOKENS_AT)
    spread = spread.reshape((n_far, n_near, n_y * n_core) + latent_grad.shape)

    latent_rows, far_latent_rows, inner = inner_products(at, spread, hidden, lat)
    far_inner = turned(inner, "far", 1)
    term_in = block_backward(
        latent_rows,
        through,
        hidden_slope,
        token_rows,
        far_latent_rows,
        far_through,
        far_slope,
        far_rows,
    )
    both = jnp.concatenate([inner, far_inner])
    both = jnp.broadcast_to(both, (n_near * n_z,) + both.shape)
    sent = jnp.concatenate([term_in.reshape(n_near * n_z, d_dev, half), both], axis=1)
    came = exchanged(sent, PAIR_ROWS).reshape(n_near, n_z, d_dev + 2 * lat, half)
    grad_in = jnp.sum(came[:, :, :d_dev].astype(F32), axis=1)
    grad_in = jnp.moveaxis(grad_in, 0, 1).reshape(d_dev, ff_mp)

    first = lax.axis_index(ROWS_AT) * d_dev
    my_final = lax.dynamic_slice_in_dim(w_final, first, d_dev, 0).astype(F32)
    my_gates = lax.dynamic_slice_in_dim(gates, first, d_dev, 1).reshape(n_z, n_far, d_dev)
    my_gates = jnp.where(far == 0, my_gates, my_gates[:, ::-1])
    my_gated = my_gates.reshape(n_images, d_dev).T[:, :, None] * my_final[:, None, :]
    my_gated = my_gated.astype(BF16).reshape(d_dev, n_images * lat)
    outs = [
        matmul(my_gated, came[at_near, :, d_dev:].reshape(n_images * lat, half))
        for at_near in range(n_near)
    ]
    return (grad_in, jnp.concatenate(outs, axis=1))


def solution(mesh):
    n_group, n_dp, n_mp = (mesh.shape[axis] for axis in ("group", "dp", "mp"))
    fine = Mesh(mesh.devices.reshape(n_group, n_dp // 2, 2, n_mp // 2, 2), AXES)
    tokens = ("y", "core")
    weights = P(ROWS_AT, tokens)
    placed = (
        P(IMAGE, tokens, None),
        P(IMAGE),
        P(),
        P(IMAGE, tokens, None),
        P(),
        weights,
        weights,
        P(),
        P(),
        P(),
        P(),
        P(None, tokens),
        P(tokens, None),
    )
    return jax.shard_map(
        on_device, mesh=fine, in_specs=placed, out_specs=(weights, weights), check_vma=False
    )
```

```python
import math

import jax
import jax.numpy as jnp
from jax import lax
from jax.experimental import pallas as pl
from jax.experimental.pallas import tpu as pltpu
from jax.sharding import Mesh
from jax.sharding import PartitionSpec as P

BF16 = jnp.bfloat16
GELU_SCALE = math.sqrt(2.0 / math.pi)
MIB = 1024 * 1024
SMALL, LARGE = 24 * MIB, 56 * MIB
F32 = jnp.float32
AXES = ("near", "z", "far", "y", "core")
IMAGE = ("z", "far")
ROWS_AT = ("near", "z", "far")
FAR_FIRST = ("far", "near", "z")
PAIR_ROWS = ("near", "z")
TOKENS_AT = ("near", "y", "core")


def layer_norm(values):
    mean = jnp.mean(values, axis=-1, keepdims=True)
    centred = values - mean
    variance = jnp.mean(centred * centred, axis=-1, keepdims=True)
    return centred * lax.rsqrt(variance + 1e-06)


def gelu_and_slope(values):
    inner = GELU_SCALE * (values + 0.044715 * values * values * values)
    bent = jnp.tanh(inner)
    half = 0.5 * (1.0 + bent)
    rate = GELU_SCALE * (1.0 + 3 * 0.044715 * values * values)
    return values * half, half + 0.5 * values * (1.0 - bent * bent) * rate


def silu_and_slope(values):
    gate = jax.nn.sigmoid(values)
    result = values * gate
    return result, gate + result * (1.0 - gate)


def norm_back(values, cotangent):
    _, pullback = jax.vjp(layer_norm, values)
    return pullback(cotangent)[0]


def matmul(left, right):
    return jnp.dot(left, right, preferred_element_type=F32)


def matmul_nt(left, right):
    return lax.dot_general(left, right, (((1,), (1,)), ((), ())), preferred_element_type=F32)


def matmul_tn(left, right):
    return lax.dot_general(left, right, (((0,), (0,)), ((), ())), preferred_element_type=F32)


def turned(value, axis, steps):
    count = lax.axis_size(axis)
    return lax.ppermute(value, axis, [(at, (at + steps) % count) for at in range(count)])


def from_all(value, axis):
    count = lax.axis_size(axis)
    return [value] + [turned(value, axis, step) for step in range(1, count)]


def summed_back(blocks, axis):
    total = blocks[0].astype(F32)
    for step in range(1, len(blocks)):
        total = total + turned(blocks[step], axis, -step).astype(F32)
    return total


def exchanged(blocks, axis):
    return lax.all_to_all(blocks, axis, 0, 0, tiled=True)


def lanes(columns):
    return pl.cdiv(columns, 128) * 128


def whole(array):
    return pl.BlockSpec(array.shape, lambda step: (0,) * len(array.shape))


SCALARS = pl.BlockSpec(memory_space=pltpu.SMEM)


def call(kernel, grid, in_specs, out_specs, out_shape, scratch, flops, moved, limit, *operands):
    return pl.pallas_call(
        kernel,
        grid=(grid,),
        in_specs=in_specs,
        out_specs=out_specs,
        out_shape=out_shape,
        scratch_shapes=scratch,
        compiler_params=pltpu.CompilerParams(vmem_limit_bytes=limit),
        cost_estimate=pl.CostEstimate(flops=flops, bytes_accessed=moved, transcendentals=0),
    )(*operands)


def block_forward_kernel(at, tokens, weights, hidden, slope):
    far = at[0]
    total = matmul(tokens[0], weights[far]) + matmul(tokens[1], weights[1 - far])
    act, rate = gelu_and_slope(total)
    columns = act.shape[1]
    hidden[...] = act.astype(BF16)
    slope[:, :columns] = rate.astype(BF16)
    if slope.shape[1] > columns:
        slope[:, columns:] = jnp.zeros((act.shape[0], slope.shape[1] - columns), BF16)


def block_forward(at, tokens, weights):
    parts, rows, width = tokens.shape
    columns = weights.shape[2]
    tile = rows // 4
    return call(
        block_forward_kernel,
        4,
        [
            SCALARS,
            pl.BlockSpec((parts, tile, width), lambda step: (0, step, 0)),
            whole(weights),
        ],
        [
            pl.BlockSpec((tile, columns), lambda step: (step, 0)),
            pl.BlockSpec((tile, lanes(columns)), lambda step: (step, 0)),
        ],
        [
            jax.ShapeDtypeStruct((rows, columns), BF16),
            jax.ShapeDtypeStruct((rows, lanes(columns)), BF16),
        ],
        [],
        2 * rows * columns * parts * width,
        2 * (parts * rows * width + parts * width * columns + 2 * rows * columns),
        LARGE,
        at,
        tokens,
        weights,
    )


def through_kernel(w_out, gated, out):
    n_near, n_images, part, _ = out.shape
    lat = gated.shape[1] // n_images
    total = matmul_tn(w_out[...], gated[...]).astype(BF16)
    for near in range(n_near):
        for image in range(n_images):
            for side in range(2):
                start = (2 * near + side) * part
                block = total[start : start + part, image * lat : (image + 1) * lat]
                out[near, image, :, side * lat : (side + 1) * lat] = block


def through_terms(w_out, gated, n_near, n_images):
    rows, columns = w_out.shape
    shape = (n_near, n_images, columns // (2 * n_near), 2 * gated.shape[1] // n_images)
    return call(
        through_kernel,
        1,
        [whole(w_out), whole(gated)],
        pl.BlockSpec(shape, lambda step: (0,) * len(shape)),
        jax.ShapeDtypeStruct(shape, BF16),
        [],
        2 * rows * columns * gated.shape[1],
        2 * rows * columns,
        LARGE,
        w_out,
        gated,
    )


def latent_kernel(at, hidden, terms, own_part, out, through, total):
    n_near, n_y, n_core, _, mine, _ = out.shape
    part, lat = terms.shape[1], through.shape[1]
    near, place = at[1], at[2]
    added = terms[0].astype(F32)
    for source in range(1, terms.shape[0]):
        added = added + terms[source].astype(F32)
    through[:part] = added[:, :lat].astype(BF16)
    through[part:] = added[:, lat:].astype(BF16)
    total[...] = matmul(hidden[...], through[...])
    rows = pl.ds(pl.multiple_of((place * n_near + near) * mine, mine), mine)
    total[rows] += own_part[pl.ds(pl.multiple_of(near * mine, mine), mine)]
    for y in range(n_y):
        for core in range(n_core):
            for side in range(n_near):
                start = ((y * n_core + core) * n_near + side) * mine
                block = total[start : start + mine].astype(BF16)
                for other in range(n_y):
                    out[side, other, core, y // 2, :, y % 2 * lat : (y % 2 + 1) * lat] = block


def latent_parts_of(at, hidden, terms, own_part, shape):
    rows, columns = hidden.shape
    lat = terms.shape[2] // 2
    return call(
        latent_kernel,
        1,
        [SCALARS, whole(hidden), whole(terms), whole(own_part)],
        [
            pl.BlockSpec(shape, lambda step: (0,) * len(shape)),
            pl.BlockSpec((columns, lat), lambda step: (0, 0)),
        ],
        [jax.ShapeDtypeStruct(shape, BF16), jax.ShapeDtypeStruct((columns, lat), BF16)],
        [pltpu.VMEM((rows, lat), F32)],
        2 * rows * columns * lat,
        2 * rows * columns,
        LARGE,
        at,
        hidden,
        terms,
        own_part,
    )


def inner_kernel(at, spread, hidden, grads, far_grads, inner):
    _, n_near, n_mp, mine, _ = spread.shape
    for image, result in ((at[0], grads), (1 - at[0], far_grads)):
        for place in range(n_mp):
            for near in range(n_near):
                start = (place * n_near + near) * mine
                result[start : start + mine] = spread[image, near, place]
    inner[...] = matmul_tn(grads[:, : inner.shape[0]], hidden[...]).astype(BF16)


def inner_products(at, spread, hidden, lat):
    rows, columns = hidden.shape
    shapes = [
        jax.ShapeDtypeStruct((rows, spread.shape[-1]), BF16),
        jax.ShapeDtypeStruct((rows, spread.shape[-1]), BF16),
        jax.ShapeDtypeStruct((lat, columns), BF16),
    ]
    return call(
        inner_kernel,
        1,
        [SCALARS, whole(spread), whole(hidden)],
        [whole(shape) for shape in shapes],
        shapes,
        [],
        2 * rows * columns * lat,
        2 * rows * columns,
        SMALL,
        at,
        spread,
        hidden,
    )


def block_backward_kernel(
    grads, through, slope, tokens, grads2, through2, slope2, tokens2, term, pre, pre2
):
    @pl.when(pl.program_id(0) == 0)
    def _():
        columns, lat = through.shape
        for grad, via, rate, result in (
            (grads, through, slope, pre),
            (grads2, through2, slope2, pre2),
        ):
            back = matmul_nt(grad[:, :lat], via[...])
            result[...] = (rate[:, :columns].astype(F32) * back).astype(BF16)

    total = matmul_tn(tokens[0], pre[...]) + matmul_tn(tokens2[...], pre2[...])
    term[...] = total.astype(BF16)


def block_backward(grads, through, slope, tokens, grads2, through2, slope2, tokens2):
    rows, width = tokens2.shape
    columns = through.shape[0]
    tile = min(640, width)
    return call(
        block_backward_kernel,
        pl.cdiv(width, tile),
        [
            whole(grads),
            whole(through),
            whole(slope),
            pl.BlockSpec((1, rows, tile), lambda step: (0, 0, step)),
            whole(grads2),
            whole(through2),
            whole(slope2),
            pl.BlockSpec((rows, tile), lambda step: (0, step)),
        ],
        pl.BlockSpec((tile, columns), lambda step: (step, 0)),
        jax.ShapeDtypeStruct((width, columns), BF16),
        [pltpu.VMEM((rows, columns), BF16)] * 2,
        4 * rows * columns * width,
        2 * (2 * rows * width + width * columns + 2 * rows * columns),
        LARGE,
        grads,
        through,
        slope,
        tokens,
        grads2,
        through2,
        slope2,
        tokens2,
    )


def decode_kernel(at, parts, w_dec1, w_dec2, w_patch, normed, embedded, slope, pixels, total, latent):
    step = pl.program_id(0)

    @pl.when(step == 0)
    def _():
        n_parts, pairs, mine, _ = parts.shape
        count = total.shape[0]
        lat = total.shape[2]
        added = parts[0].astype(F32)
        for source in range(1, n_parts):
            added = added + parts[source].astype(F32)
        for pair in range(pairs):
            total[2 * pair] = added[pair, :, :lat]
            total[2 * pair + 1] = added[pair, :, lat:]
        for turn in range(count):
            owner = lax.rem(at[3] - turn + count, count)
            latent[turn * mine : (turn + 1) * mine] = total[owner].astype(BF16)

    act, rate = silu_and_slope(matmul(latent[...], w_dec1[...]))
    slope[...] = rate[: slope.shape[0]]
    part = matmul(act.astype(BF16), w_dec2[...])

    @pl.when(step == 0)
    def _():
        pixels[...] = part

    @pl.when(step > 0)
    def _():
        pixels[...] += part

    @pl.when(step == pl.num_programs(0) - 1)
    def _():
        patches = matmul(pixels[...].astype(BF16), w_patch[...])
        normed[...] = layer_norm(patches).astype(BF16)
        embedded[...] = patches[: embedded.shape[0]]


def decode(at, parts, w_dec1, w_dec2, w_patch, mine):
    count, lat = 2 * parts.shape[1], parts.shape[3] // 2
    rows = count * mine
    deep, pix = w_dec2.shape
    width = w_patch.shape[1]
    tile = min(512, deep)
    return call(
        decode_kernel,
        deep // tile,
        [
            SCALARS,
            whole(parts),
            pl.BlockSpec((lat, tile), lambda step: (0, step)),
            pl.BlockSpec((tile, pix), lambda step: (step, 0)),
            whole(w_patch),
        ],
        [
            pl.BlockSpec((rows, width), lambda step: (0, 0)),
            pl.BlockSpec((mine, width), lambda step: (0, 0)),
            pl.BlockSpec((mine, tile), lambda step: (0, step)),
        ],
        [
            jax.ShapeDtypeStruct((rows, width), BF16),
            jax.ShapeDtypeStruct((mine, width), F32),
            jax.ShapeDtypeStruct((mine, deep), F32),
        ],
        [
            pltpu.VMEM((rows, pix), F32),
            pltpu.VMEM((count, mine, lat), F32),
            pltpu.VMEM((rows, lat), BF16),
        ],
        2 * rows * (lat * deep + deep * pix + pix * width),
        2 * (deep * pix + pix * width),
        SMALL,
        at,
        parts,
        w_dec1,
        w_dec2,
        w_patch,
    )


def reward_forward_kernel(normed, v1a, v1b, v2a, v2b, slope_a, slope_b, out, total):
    step = pl.program_id(0)
    part = 0.0
    for v1, v2, slope in ((v1a, v2a, slope_a), (v1b, v2b, slope_b)):
        act, rate = gelu_and_slope(matmul(normed[...], v1[...]))
        slope[...] = rate
        part = part + matmul(act.astype(BF16), v2[...])

    @pl.when(step == 0)
    def _():
        total[...] = part

    @pl.when(step > 0)
    def _():
        total[...] += part

    @pl.when(step == pl.num_programs(0) - 1)
    def _():
        out[...] = total[...].astype(BF16)


def reward_backward_kernel(grad, v1a, v1b, v2a, v2b, slope_a, slope_b, out, total):
    step = pl.program_id(0)
    part = 0.0
    for v1, v2, slope in ((v1a, v2a, slope_a), (v1b, v2b, slope_b)):
        back = (slope[...] * matmul_nt(grad[...], v2[...])).astype(BF16)
        part = part + matmul_nt(back, v1[...])

    @pl.when(step == 0)
    def _():
        total[...] = part

    @pl.when(step > 0)
    def _():
        total[...] += part

    @pl.when(step == pl.num_programs(0) - 1)
    def _():
        out[...] = total[...].astype(BF16)


def reward(values, v1_both, v2_both, slopes=None):
    rows, width = values.shape
    hidden = v1_both[0].shape[1]
    tile = hidden
    slope_spec = pl.BlockSpec((rows, tile), lambda step: (0, step))
    slope_shape = jax.ShapeDtypeStruct((rows, hidden), F32)
    out_spec = pl.BlockSpec((rows, width), lambda step: (0, 0))
    out_shape = jax.ShapeDtypeStruct((rows, width), BF16)
    v1_spec = pl.BlockSpec((width, tile), lambda step: (0, step))
    v2_spec = pl.BlockSpec((tile, width), lambda step: (step, 0))
    weight_specs = [whole(values), v1_spec, v1_spec, v2_spec, v2_spec]
    forward = slopes is None
    return call(
        reward_forward_kernel if forward else reward_backward_kernel,
        hidden // tile,
        weight_specs + ([] if forward else [slope_spec] * 2),
        [slope_spec] * 2 + [out_spec] if forward else out_spec,
        [slope_shape] * 2 + [out_shape] if forward else out_shape,
        [pltpu.VMEM((rows, width), F32)],
        8 * rows * width * hidden,
        8 * width * hidden,
        SMALL,
        values,
        *v1_both,
        *v2_both,
        *(() if forward else slopes),
    )


def on_device(
    latent_noise,
    timestep,
    reward_slot,
    target,
    modulation,
    w_in,
    w_out_t,
    w_final,
    w_dec1,
    w_dec2,
    w_patch,
    w_v1,
    w_v2,
):
    tok_dev = latent_noise.shape[1]
    n_near, n_y, n_core = (lax.axis_size(axis) for axis in TOKENS_AT)
    n_images = lax.axis_size("z") * lax.axis_size("far")
    n_rows = n_near * n_images
    n_tokens = n_near * n_y * n_core
    mine = tok_dev // n_near
    rows = tok_dev * n_y * n_core
    d_dev, ff_mp = w_in.shape
    width_d = d_dev * n_rows
    half = ff_mp // n_near
    lat = w_final.shape[1]
    scale = 1.0 / math.sqrt(n_images * rows)
    near = lax.axis_index("near")
    my_image = lax.axis_index(IMAGE)
    my_slot = reward_slot[my_image]

    n_z, n_far = lax.axis_size("z"), lax.axis_size("far")
    far = lax.axis_index("far")
    wide = width_d // n_far

    at = jnp.stack([far, near, lax.axis_index(("y", "core")), lax.axis_index("y")]).astype(jnp.int32)

    turned_steps = from_all(timestep, IMAGE)
    images = lax.iota(jnp.int32, n_images)
    all_steps = jnp.zeros_like(images)
    for step, value in enumerate(turned_steps):
        all_steps = jnp.where(images == (my_image - step) % n_images, value[0], all_steps)

    split_in = jnp.moveaxis(w_in.reshape(d_dev, n_near, half), 1, 0)
    split_in = jnp.broadcast_to(split_in[None, :, None], (n_far, n_near, n_z, d_dev, half))
    split_in = split_in.reshape(n_rows, d_dev, half)
    split_in, all_steps = lax.optimization_barrier((split_in, all_steps))
    full_in = exchanged(split_in, FAR_FIRST).reshape(n_far, wide, half)

    noise_rows = latent_noise[0]
    modulate = modulation[timestep[0]]
    modulated = (
        layer_norm(noise_rows.astype(F32)) * (1.0 + modulate[1]) + modulate[0]
    ).astype(BF16)
    modulated = modulated.reshape(tok_dev, n_rows // n_far, n_far, d_dev)
    modulated = jnp.moveaxis(modulated, 2, 0).reshape(n_far, tok_dev, wide)
    modulated = jnp.where(far == 0, modulated, modulated[::-1])
    token_rows = lax.all_gather(modulated, ("y", "core"), axis=1, tiled=True)
    far_rows = lax.all_gather(turned(modulated[1], "far", 1), ("y", "core"), axis=0, tiled=True)

    first = lax.axis_index(ROWS_AT) * d_dev
    my_final = lax.dynamic_slice_in_dim(w_final, first, d_dev, 0).astype(F32)
    gates = jnp.stack(
        [
            lax.dynamic_slice(modulation, (all_steps[image], 2, first), (1, 1, d_dev))[0, 0]
            for image in range(n_images)
        ]
    )
    gated = (gates.T[:, :, None] * my_final[:, None, :]).astype(BF16)
    terms = through_terms(w_out_t, gated.reshape(d_dev, n_images * lat), n_near, n_images)
    terms = terms.reshape((n_rows,) + terms.shape[2:])
    terms, full_in, own_target = lax.optimization_barrier((terms, full_in, target[0]))
    terms = exchanged(terms, ROWS_AT)

    v1_both = (w_v1, turned(w_v1, "core", 1))
    v2_both = (w_v2, turned(w_v2, "core", 1))

    hidden, hidden_slope = block_forward(at, token_rows, full_in)
    own_target = lax.dynamic_slice_in_dim(own_target, near * mine, mine, 0)
    own_target = jnp.pad(own_target, ((0, mine // 6), (0, 0)))
    goals = lax.all_gather(own_target, IMAGE, axis=0)
    goal = lax.dynamic_index_in_dim(goals, my_slot, 0, keepdims=False)[:mine]
    goal = goal.astype(F32)
    far_slope = turned(hidden_slope, "far", 1)
    own_part = matmul(noise_rows, w_final)
    shape = (n_near, n_y, n_core, n_y // 2, mine, 2 * lat)
    latent_part, through = latent_parts_of(at, hidden, terms, own_part, shape)
    far_through = turned(through, "far", 1)
    latent_parts = exchanged(latent_part.reshape(n_tokens, n_y // 2, mine, 2 * lat), TOKENS_AT)

    patch_rows, embedded, dec_slope = decode(at, latent_parts, w_dec1, w_dec2, w_patch, mine)
    *slopes, vit_part = reward(patch_rows, v1_both, v2_both)
    vit_out = summed_back(jnp.split(vit_part, n_y), "y")
    feature_grad = ((embedded + vit_out - goal) * scale).astype(BF16)

    grad_rows = jnp.concatenate(from_all(feature_grad, "y"))
    norm_part = reward(grad_rows, v1_both, v2_both, slopes)
    norm_grad = summed_back(jnp.split(norm_part, n_y), "y")
    norm_grad, far_slope, far_through = lax.optimization_barrier(
        (norm_grad, far_slope, far_through)
    )
    embed_grad = (feature_grad.astype(F32) + norm_back(embedded, norm_grad)).astype(BF16)
    pixel_grad = matmul_nt(embed_grad, w_patch).astype(BF16)
    dec_pre_grad = (dec_slope * matmul_nt(pixel_grad, w_dec2)).astype(BF16)
    latent_grad = matmul_nt(dec_pre_grad, w_dec1).astype(BF16)

    latent_grad = jnp.pad(latent_grad, ((0, 0), (0, lanes(lat) - lat)))
    spread = jnp.broadcast_to(latent_grad, (n_far * n_tokens,) + latent_grad.shape)
    spread = exchanged(spread, ("far",) + TOKENS_AT)
    spread = spread.reshape((n_far, n_near, n_y * n_core) + latent_grad.shape)

    latent_rows, far_latent_rows, inner = inner_products(at, spread, hidden, lat)
    far_inner = turned(inner, "far", 1)
    term_in = block_backward(
        latent_rows,
        through,
        hidden_slope,
        token_rows,
        far_latent_rows,
        far_through,
        far_slope,
        far_rows,
    )
    both = jnp.concatenate([inner, far_inner])
    both = jnp.broadcast_to(both, (n_near * n_z,) + both.shape)
    sent = jnp.concatenate([term_in.reshape(n_near * n_z, d_dev, half), both], axis=1)
    came = exchanged(sent, PAIR_ROWS).reshape(n_near, n_z, d_dev + 2 * lat, half)
    grad_in = jnp.sum(came[:, :, :d_dev].astype(F32), axis=1)
    grad_in = jnp.moveaxis(grad_in, 0, 1).reshape(d_dev, ff_mp)

    my_gated = gated.reshape(d_dev, n_z, n_far, lat)
    my_gated = jnp.where(far == 0, my_gated, my_gated[:, :, ::-1]).reshape(d_dev, n_images * lat)
    outs = [
        matmul(my_gated, came[at_near, :, d_dev:].reshape(n_images * lat, half))
        for at_near in range(n_near)
    ]
    return (grad_in, jnp.concatenate(outs, axis=1))


def solution(mesh):
    n_group, n_dp, n_mp = (mesh.shape[axis] for axis in ("group", "dp", "mp"))
    fine = Mesh(mesh.devices.reshape(n_group, n_dp // 2, 2, n_mp // 2, 2), AXES)
    tokens = ("y", "core")
    weights = P(ROWS_AT, tokens)
    placed = (
        P(IMAGE, tokens, None),
        P(IMAGE),
        P(),
        P(IMAGE, tokens, None),
        P(),
        weights,
        weights,
        P(),
        P(),
        P(),
        P(),
        P(None, tokens),
        P(tokens, None),
    )
    return jax.shard_map(
        on_device, mesh=fine, in_specs=placed, out_specs=(weights, weights), check_vma=False
    )
```

```python
import math

import jax
import jax.numpy as jnp
from jax import lax
from jax.experimental import pallas as pl
from jax.experimental.pallas import tpu as pltpu
from jax.sharding import Mesh
from jax.sharding import PartitionSpec as P

BF16 = jnp.bfloat16
GELU_SCALE = math.sqrt(2.0 / math.pi)
MIB = 1024 * 1024
SMALL, LARGE = 24 * MIB, 56 * MIB
F32 = jnp.float32
AXES = ("near", "z", "far", "y", "core")
IMAGE = ("z", "far")
ROWS_AT = ("near", "z", "far")
FAR_FIRST = ("far", "near", "z")
PAIR_ROWS = ("near", "z")
TOKENS_AT = ("near", "y", "core")


def layer_norm(values):
    mean = jnp.mean(values, axis=-1, keepdims=True)
    centred = values - mean
    variance = jnp.mean(centred * centred, axis=-1, keepdims=True)
    return centred * lax.rsqrt(variance + 1e-06)


def gelu_and_slope(values):
    inner = GELU_SCALE * (values + 0.044715 * values * values * values)
    bent = jnp.tanh(inner)
    half = 0.5 * (1.0 + bent)
    rate = GELU_SCALE * (1.0 + 3 * 0.044715 * values * values)
    return values * half, half + 0.5 * values * (1.0 - bent * bent) * rate


def silu_and_slope(values):
    gate = jax.nn.sigmoid(values)
    result = values * gate
    return result, gate + result * (1.0 - gate)


def norm_back(values, cotangent):
    _, pullback = jax.vjp(layer_norm, values)
    return pullback(cotangent)[0]


def matmul(left, right):
    return jnp.dot(left, right, preferred_element_type=F32)


def matmul_nt(left, right):
    return lax.dot_general(left, right, (((1,), (1,)), ((), ())), preferred_element_type=F32)


def matmul_tn(left, right):
    return lax.dot_general(left, right, (((0,), (0,)), ((), ())), preferred_element_type=F32)


def turned(value, axis, steps):
    count = lax.axis_size(axis)
    return lax.ppermute(value, axis, [(at, (at + steps) % count) for at in range(count)])


def from_all(value, axis):
    count = lax.axis_size(axis)
    return [value] + [turned(value, axis, step) for step in range(1, count)]


def summed_back(blocks, axis):
    total = blocks[0].astype(F32)
    for step in range(1, len(blocks)):
        total = total + turned(blocks[step], axis, -step).astype(F32)
    return total


def exchanged(blocks, axis):
    return lax.all_to_all(blocks, axis, 0, 0, tiled=True)


def lanes(columns):
    return pl.cdiv(columns, 128) * 128


def whole(array):
    return pl.BlockSpec(array.shape, lambda step: (0,) * len(array.shape))


SCALARS = pl.BlockSpec(memory_space=pltpu.SMEM)


def call(kernel, grid, in_specs, out_specs, out_shape, scratch, flops, moved, limit, *operands):
    return pl.pallas_call(
        kernel,
        grid=(grid,),
        in_specs=in_specs,
        out_specs=out_specs,
        out_shape=out_shape,
        scratch_shapes=scratch,
        compiler_params=pltpu.CompilerParams(vmem_limit_bytes=limit),
        cost_estimate=pl.CostEstimate(flops=flops, bytes_accessed=moved, transcendentals=0),
    )(*operands)


def block_forward_kernel(at, tokens, weights, hidden, slope):
    far = at[0]
    total = matmul(tokens[0], weights[far]) + matmul(tokens[1], weights[1 - far])
    act, rate = gelu_and_slope(total)
    columns = act.shape[1]
    hidden[...] = act.astype(BF16)
    slope[:, :columns] = rate.astype(BF16)
    if slope.shape[1] > columns:
        slope[:, columns:] = jnp.zeros((act.shape[0], slope.shape[1] - columns), BF16)


def block_forward(at, tokens, weights):
    parts, rows, width = tokens.shape
    columns = weights.shape[2]
    tile = rows // 4
    return call(
        block_forward_kernel,
        4,
        [
            SCALARS,
            pl.BlockSpec((parts, tile, width), lambda step: (0, step, 0)),
            whole(weights),
        ],
        [
            pl.BlockSpec((tile, columns), lambda step: (step, 0)),
            pl.BlockSpec((tile, lanes(columns)), lambda step: (step, 0)),
        ],
        [
            jax.ShapeDtypeStruct((rows, columns), BF16),
            jax.ShapeDtypeStruct((rows, lanes(columns)), BF16),
        ],
        [],
        2 * rows * columns * parts * width,
        2 * (parts * rows * width + parts * width * columns + 2 * rows * columns),
        LARGE,
        at,
        tokens,
        weights,
    )


def through_kernel(w_out, gated, out):
    n_near, n_images, part, _ = out.shape
    lat = gated.shape[1] // n_images
    total = matmul_tn(w_out[...], gated[...]).astype(BF16)
    for near in range(n_near):
        for image in range(n_images):
            for side in range(2):
                start = (2 * near + side) * part
                block = total[start : start + part, image * lat : (image + 1) * lat]
                out[near, image, :, side * lat : (side + 1) * lat] = block


def through_terms(w_out, gated, n_near, n_images):
    rows, columns = w_out.shape
    shape = (n_near, n_images, columns // (2 * n_near), 2 * gated.shape[1] // n_images)
    return call(
        through_kernel,
        1,
        [whole(w_out), whole(gated)],
        pl.BlockSpec(shape, lambda step: (0,) * len(shape)),
        jax.ShapeDtypeStruct(shape, BF16),
        [],
        2 * rows * columns * gated.shape[1],
        2 * rows * columns,
        LARGE,
        w_out,
        gated,
    )


def latent_kernel(at, hidden, terms, own_part, out, through, total):
    n_near, n_y, n_core, _, mine, _ = out.shape
    part, lat = terms.shape[1], through.shape[1]
    near, place = at[1], at[2]
    added = terms[0].astype(F32)
    for source in range(1, terms.shape[0]):
        added = added + terms[source].astype(F32)
    through[:part] = added[:, :lat].astype(BF16)
    through[part:] = added[:, lat:].astype(BF16)
    total[...] = matmul(hidden[...], through[...])
    rows = pl.ds(pl.multiple_of((place * n_near + near) * mine, mine), mine)
    total[rows] += own_part[pl.ds(pl.multiple_of(near * mine, mine), mine)]
    for y in range(n_y):
        for core in range(n_core):
            for side in range(n_near):
                start = ((y * n_core + core) * n_near + side) * mine
                block = total[start : start + mine].astype(BF16)
                for other in range(n_y):
                    out[side, other, core, y // 2, :, y % 2 * lat : (y % 2 + 1) * lat] = block


def latent_parts_of(at, hidden, terms, own_part, shape):
    rows, columns = hidden.shape
    lat = terms.shape[2] // 2
    return call(
        latent_kernel,
        1,
        [SCALARS, whole(hidden), whole(terms), whole(own_part)],
        [
            pl.BlockSpec(shape, lambda step: (0,) * len(shape)),
            pl.BlockSpec((columns, lat), lambda step: (0, 0)),
        ],
        [jax.ShapeDtypeStruct(shape, BF16), jax.ShapeDtypeStruct((columns, lat), BF16)],
        [pltpu.VMEM((rows, lat), F32)],
        2 * rows * columns * lat,
        2 * rows * columns,
        LARGE,
        at,
        hidden,
        terms,
        own_part,
    )


def inner_kernel(spread, hidden, grads, far_grads, inner):
    n_near, n_mp, _, mine, _ = spread.shape
    for image, result in ((0, grads), (1, far_grads)):
        for place in range(n_mp):
            for near in range(n_near):
                start = (place * n_near + near) * mine
                result[start : start + mine] = spread[near, place, image]
    inner[...] = matmul_tn(grads[:, : inner.shape[0]], hidden[...]).astype(BF16)


def inner_products(spread, hidden, lat):
    rows, columns = hidden.shape
    shapes = [
        jax.ShapeDtypeStruct((rows, spread.shape[-1]), BF16),
        jax.ShapeDtypeStruct((rows, spread.shape[-1]), BF16),
        jax.ShapeDtypeStruct((lat, columns), BF16),
    ]
    return call(
        inner_kernel,
        1,
        [whole(spread), whole(hidden)],
        [whole(shape) for shape in shapes],
        shapes,
        [],
        2 * rows * columns * lat,
        2 * rows * columns,
        SMALL,
        spread,
        hidden,
    )


def block_backward_kernel(
    grads, through, slope, tokens, grads2, through2, slope2, tokens2, term, pre, pre2
):
    @pl.when(pl.program_id(0) == 0)
    def _():
        columns, lat = through.shape
        for grad, via, rate, result in (
            (grads, through, slope, pre),
            (grads2, through2, slope2, pre2),
        ):
            back = matmul_nt(grad[:, :lat], via[...])
            result[...] = (rate[:, :columns].astype(F32) * back).astype(BF16)

    total = matmul_tn(tokens[0], pre[...]) + matmul_tn(tokens2[...], pre2[...])
    term[...] = total.astype(BF16)


def block_backward(grads, through, slope, tokens, grads2, through2, slope2, tokens2):
    rows, width = tokens2.shape
    columns = through.shape[0]
    tile = min(640, width)
    return call(
        block_backward_kernel,
        pl.cdiv(width, tile),
        [
            whole(grads),
            whole(through),
            whole(slope),
            pl.BlockSpec((1, rows, tile), lambda step: (0, 0, step)),
            whole(grads2),
            whole(through2),
            whole(slope2),
            pl.BlockSpec((rows, tile), lambda step: (0, step)),
        ],
        pl.BlockSpec((tile, columns), lambda step: (step, 0)),
        jax.ShapeDtypeStruct((width, columns), BF16),
        [pltpu.VMEM((rows, columns), BF16)] * 2,
        4 * rows * columns * width,
        2 * (2 * rows * width + width * columns + 2 * rows * columns),
        LARGE,
        grads,
        through,
        slope,
        tokens,
        grads2,
        through2,
        slope2,
        tokens2,
    )


def decode_kernel(at, parts, w_dec1, w_dec2, w_patch, normed, embedded, slope, pixels, total, latent):
    step = pl.program_id(0)

    @pl.when(step == 0)
    def _():
        n_parts, pairs, mine, _ = parts.shape
        count = total.shape[0]
        lat = total.shape[2]
        added = parts[0].astype(F32)
        for source in range(1, n_parts):
            added = added + parts[source].astype(F32)
        for pair in range(pairs):
            total[2 * pair] = added[pair, :, :lat]
            total[2 * pair + 1] = added[pair, :, lat:]
        for turn in range(count):
            owner = lax.rem(at[3] - turn + count, count)
            latent[turn * mine : (turn + 1) * mine] = total[owner].astype(BF16)

    act, rate = silu_and_slope(matmul(latent[...], w_dec1[...]))
    slope[...] = rate[: slope.shape[0]]
    part = matmul(act.astype(BF16), w_dec2[...])

    @pl.when(step == 0)
    def _():
        pixels[...] = part

    @pl.when(step > 0)
    def _():
        pixels[...] += part

    @pl.when(step == pl.num_programs(0) - 1)
    def _():
        patches = matmul(pixels[...].astype(BF16), w_patch[...])
        normed[...] = layer_norm(patches).astype(BF16)
        embedded[...] = patches[: embedded.shape[0]]


def decode(at, parts, w_dec1, w_dec2, w_patch, mine):
    count, lat = 2 * parts.shape[1], parts.shape[3] // 2
    rows = count * mine
    deep, pix = w_dec2.shape
    width = w_patch.shape[1]
    tile = min(512, deep)
    return call(
        decode_kernel,
        deep // tile,
        [
            SCALARS,
            whole(parts),
            pl.BlockSpec((lat, tile), lambda step: (0, step)),
            pl.BlockSpec((tile, pix), lambda step: (step, 0)),
            whole(w_patch),
        ],
        [
            pl.BlockSpec((rows, width), lambda step: (0, 0)),
            pl.BlockSpec((mine, width), lambda step: (0, 0)),
            pl.BlockSpec((mine, tile), lambda step: (0, step)),
        ],
        [
            jax.ShapeDtypeStruct((rows, width), BF16),
            jax.ShapeDtypeStruct((mine, width), F32),
            jax.ShapeDtypeStruct((mine, deep), F32),
        ],
        [
            pltpu.VMEM((rows, pix), F32),
            pltpu.VMEM((count, mine, lat), F32),
            pltpu.VMEM((rows, lat), BF16),
        ],
        2 * rows * (lat * deep + deep * pix + pix * width),
        2 * (deep * pix + pix * width),
        SMALL,
        at,
        parts,
        w_dec1,
        w_dec2,
        w_patch,
    )


def reward_forward_kernel(normed, v1a, v1b, v2a, v2b, slope_a, slope_b, out, total):
    step = pl.program_id(0)
    part = 0.0
    for v1, v2, slope in ((v1a, v2a, slope_a), (v1b, v2b, slope_b)):
        act, rate = gelu_and_slope(matmul(normed[...], v1[...]))
        slope[...] = rate
        part = part + matmul(act.astype(BF16), v2[...])

    @pl.when(step == 0)
    def _():
        total[...] = part

    @pl.when(step > 0)
    def _():
        total[...] += part

    @pl.when(step == pl.num_programs(0) - 1)
    def _():
        out[...] = total[...].astype(BF16)


def reward_backward_kernel(grad, v1a, v1b, v2a, v2b, slope_a, slope_b, out, total):
    step = pl.program_id(0)
    part = 0.0
    for v1, v2, slope in ((v1a, v2a, slope_a), (v1b, v2b, slope_b)):
        back = (slope[...] * matmul_nt(grad[...], v2[...])).astype(BF16)
        part = part + matmul_nt(back, v1[...])

    @pl.when(step == 0)
    def _():
        total[...] = part

    @pl.when(step > 0)
    def _():
        total[...] += part

    @pl.when(step == pl.num_programs(0) - 1)
    def _():
        out[...] = total[...].astype(BF16)


def reward(values, v1_both, v2_both, slopes=None):
    rows, width = values.shape
    hidden = v1_both[0].shape[1]
    tile = hidden
    slope_spec = pl.BlockSpec((rows, tile), lambda step: (0, step))
    slope_shape = jax.ShapeDtypeStruct((rows, hidden), F32)
    out_spec = pl.BlockSpec((rows, width), lambda step: (0, 0))
    out_shape = jax.ShapeDtypeStruct((rows, width), BF16)
    v1_spec = pl.BlockSpec((width, tile), lambda step: (0, step))
    v2_spec = pl.BlockSpec((tile, width), lambda step: (step, 0))
    weight_specs = [whole(values), v1_spec, v1_spec, v2_spec, v2_spec]
    forward = slopes is None
    return call(
        reward_forward_kernel if forward else reward_backward_kernel,
        hidden // tile,
        weight_specs + ([] if forward else [slope_spec] * 2),
        [slope_spec] * 2 + [out_spec] if forward else out_spec,
        [slope_shape] * 2 + [out_shape] if forward else out_shape,
        [pltpu.VMEM((rows, width), F32)],
        8 * rows * width * hidden,
        8 * width * hidden,
        SMALL,
        values,
        *v1_both,
        *v2_both,
        *(() if forward else slopes),
    )


def on_device(
    latent_noise,
    timestep,
    reward_slot,
    target,
    modulation,
    w_in,
    w_out_t,
    w_final,
    w_dec1,
    w_dec2,
    w_patch,
    w_v1,
    w_v2,
):
    tok_dev = latent_noise.shape[1]
    n_near, n_y, n_core = (lax.axis_size(axis) for axis in TOKENS_AT)
    n_images = lax.axis_size("z") * lax.axis_size("far")
    n_rows = n_near * n_images
    n_tokens = n_near * n_y * n_core
    mine = tok_dev // n_near
    rows = tok_dev * n_y * n_core
    d_dev, ff_mp = w_in.shape
    width_d = d_dev * n_rows
    half = ff_mp // n_near
    lat = w_final.shape[1]
    scale = 1.0 / math.sqrt(n_images * rows)
    near = lax.axis_index("near")
    my_image = lax.axis_index(IMAGE)
    my_slot = reward_slot[my_image]

    n_z, n_far = lax.axis_size("z"), lax.axis_size("far")
    far = lax.axis_index("far")
    wide = width_d // n_far

    at = jnp.stack([far, near, lax.axis_index(("y", "core")), lax.axis_index("y")]).astype(jnp.int32)

    far_step = turned(timestep, "far", 1)
    pair_steps = jnp.where(far == 0, jnp.stack([timestep, far_step]), jnp.stack([far_step, timestep]))
    turned_steps = from_all(pair_steps, "z")

    split_in = jnp.moveaxis(w_in.reshape(d_dev, n_near, half), 1, 0)
    split_in = jnp.broadcast_to(split_in[None, :, None], (n_far, n_near, n_z, d_dev, half))
    split_in = split_in.reshape(n_rows, d_dev, half)
    split_in, turned_steps = lax.optimization_barrier((split_in, turned_steps))
    full_in = exchanged(split_in, FAR_FIRST).reshape(n_far, wide, half)

    noise_rows = latent_noise[0]
    modulate = modulation[timestep[0]]
    modulated = (
        layer_norm(noise_rows.astype(F32)) * (1.0 + modulate[1]) + modulate[0]
    ).astype(BF16)
    modulated = modulated.reshape(tok_dev, n_rows // n_far, n_far, d_dev)
    modulated = jnp.moveaxis(modulated, 2, 0).reshape(n_far, tok_dev, wide)
    modulated = jnp.where(far == 0, modulated, modulated[::-1])
    token_rows = lax.all_gather(modulated, ("y", "core"), axis=1, tiled=True)
    far_rows = lax.all_gather(turned(modulated[1], "far", 1), ("y", "core"), axis=0, tiled=True)

    all_steps = jnp.zeros((n_z, n_far), jnp.int32)
    for step, value in enumerate(turned_steps):
        owner = (lax.axis_index("z") - step) % n_z
        here = lax.broadcasted_iota(jnp.int32, (n_z, n_far), 0) == owner
        all_steps = jnp.where(here, value.reshape(1, n_far), all_steps)
    all_steps = all_steps.reshape(n_images)

    first = lax.axis_index(ROWS_AT) * d_dev
    my_final = lax.dynamic_slice_in_dim(w_final, first, d_dev, 0).astype(F32)
    gates = jnp.stack(
        [
            lax.dynamic_slice(modulation, (all_steps[image], 2, first), (1, 1, d_dev))[0, 0]
            for image in range(n_images)
        ]
    )
    gated = (gates.T[:, :, None] * my_final[:, None, :]).astype(BF16)
    terms = through_terms(w_out_t, gated.reshape(d_dev, n_images * lat), n_near, n_images)
    terms = terms.reshape((n_rows,) + terms.shape[2:])
    terms, full_in, own_target = lax.optimization_barrier((terms, full_in, target[0]))
    terms = exchanged(terms, ROWS_AT)

    v1_both = (w_v1, turned(w_v1, "core", 1))
    v2_both = (w_v2, turned(w_v2, "core", 1))

    hidden, hidden_slope = block_forward(at, token_rows, full_in)
    own_target = lax.dynamic_slice_in_dim(own_target, near * mine, mine, 0)
    own_target = jnp.pad(own_target, ((0, mine // 6), (0, 0)))
    goals = lax.all_gather(own_target, IMAGE, axis=0)
    goal = lax.dynamic_index_in_dim(goals, my_slot, 0, keepdims=False)[:mine]
    goal = goal.astype(F32)
    far_slope = turned(hidden_slope, "far", 1)
    own_part = matmul(noise_rows, w_final)
    shape = (n_near, n_y, n_core, n_y // 2, mine, 2 * lat)
    latent_part, through = latent_parts_of(at, hidden, terms, own_part, shape)
    far_through = turned(through, "far", 1)
    latent_parts = exchanged(latent_part.reshape(n_tokens, n_y // 2, mine, 2 * lat), TOKENS_AT)

    patch_rows, embedded, dec_slope = decode(at, latent_parts, w_dec1, w_dec2, w_patch, mine)
    *slopes, vit_part = reward(patch_rows, v1_both, v2_both)
    vit_out = summed_back(jnp.split(vit_part, n_y), "y")
    feature_grad = ((embedded + vit_out - goal) * scale).astype(BF16)

    grad_rows = jnp.concatenate(from_all(feature_grad, "y"))
    norm_part = reward(grad_rows, v1_both, v2_both, slopes)
    norm_grad = summed_back(jnp.split(norm_part, n_y), "y")
    norm_grad, far_slope, far_through = lax.optimization_barrier(
        (norm_grad, far_slope, far_through)
    )
    embed_grad = (feature_grad.astype(F32) + norm_back(embedded, norm_grad)).astype(BF16)
    pixel_grad = matmul_nt(embed_grad, w_patch).astype(BF16)
    dec_pre_grad = (dec_slope * matmul_nt(pixel_grad, w_dec2)).astype(BF16)
    latent_grad = matmul_nt(dec_pre_grad, w_dec1).astype(BF16)

    latent_grad = jnp.pad(latent_grad, ((0, 0), (0, lanes(lat) - lat)))
    latent_grad = jnp.stack([latent_grad, turned(latent_grad, "far", 1)])
    spread = exchanged(jnp.broadcast_to(latent_grad, (n_tokens,) + latent_grad.shape), TOKENS_AT)
    spread = spread.reshape((n_near, n_y * n_core) + latent_grad.shape)

    latent_rows, far_latent_rows, inner = inner_products(spread, hidden, lat)
    far_inner = turned(inner, "far", 1)
    term_in = block_backward(
        latent_rows,
        through,
        hidden_slope,
        token_rows,
        far_latent_rows,
        far_through,
        far_slope,
        far_rows,
    )
    both = jnp.concatenate([inner, far_inner])
    both = jnp.broadcast_to(both, (n_near * n_z,) + both.shape)
    sent = jnp.concatenate([term_in.reshape(n_near * n_z, d_dev, half), both], axis=1)
    came = exchanged(sent, PAIR_ROWS).reshape(n_near, n_z, d_dev + 2 * lat, half)
    grad_in = jnp.sum(came[:, :, :d_dev].astype(F32), axis=1)
    grad_in = jnp.moveaxis(grad_in, 0, 1).reshape(d_dev, ff_mp)

    my_gated = gated.reshape(d_dev, n_z, n_far, lat)
    my_gated = jnp.where(far == 0, my_gated, my_gated[:, :, ::-1]).reshape(d_dev, n_images * lat)
    outs = [
        matmul(my_gated, came[at_near, :, d_dev:].reshape(n_images * lat, half))
        for at_near in range(n_near)
    ]
    return (grad_in, jnp.concatenate(outs, axis=1))


def solution(mesh):
    n_group, n_dp, n_mp = (mesh.shape[axis] for axis in ("group", "dp", "mp"))
    fine = Mesh(mesh.devices.reshape(n_group, n_dp // 2, 2, n_mp // 2, 2), AXES)
    tokens = ("y", "core")
    weights = P(ROWS_AT, tokens)
    placed = (
        P(IMAGE, tokens, None),
        P(IMAGE),
        P(),
        P(IMAGE, tokens, None),
        P(),
        weights,
        weights,
        P(),
        P(),
        P(),
        P(),
        P(None, tokens),
        P(tokens, None),
    )
    return jax.shard_map(
        on_device, mesh=fine, in_specs=placed, out_specs=(weights, weights), check_vma=False
    )
```

```python
import math

import jax
import jax.numpy as jnp
from jax import lax
from jax.experimental import pallas as pl
from jax.experimental.pallas import tpu as pltpu
from jax.sharding import Mesh
from jax.sharding import PartitionSpec as P

BF16 = jnp.bfloat16
GELU_SCALE = math.sqrt(2.0 / math.pi)
MIB = 1024 * 1024
SMALL, LARGE = 24 * MIB, 56 * MIB
F32 = jnp.float32
AXES = ("near", "z", "far", "y", "core")
IMAGE = ("z", "far")
ROWS_AT = ("near", "z", "far")
FAR_FIRST = ("far", "near", "z")
PAIR_ROWS = ("near", "z")
TOKENS_AT = ("near", "y", "core")


def layer_norm(values):
    mean = jnp.mean(values, axis=-1, keepdims=True)
    centred = values - mean
    variance = jnp.mean(centred * centred, axis=-1, keepdims=True)
    return centred * lax.rsqrt(variance + 1e-06)


def gelu_and_slope(values):
    inner = GELU_SCALE * (values + 0.044715 * values * values * values)
    bent = jnp.tanh(inner)
    half = 0.5 * (1.0 + bent)
    rate = GELU_SCALE * (1.0 + 3 * 0.044715 * values * values)
    return values * half, half + 0.5 * values * (1.0 - bent * bent) * rate


def silu_and_slope(values):
    gate = jax.nn.sigmoid(values)
    result = values * gate
    return result, gate + result * (1.0 - gate)


def norm_back(values, cotangent):
    _, pullback = jax.vjp(layer_norm, values)
    return pullback(cotangent)[0]


def matmul(left, right):
    return jnp.dot(left, right, preferred_element_type=F32)


def matmul_nt(left, right):
    return lax.dot_general(left, right, (((1,), (1,)), ((), ())), preferred_element_type=F32)


def matmul_tn(left, right):
    return lax.dot_general(left, right, (((0,), (0,)), ((), ())), preferred_element_type=F32)


def turned(value, axis, steps):
    count = lax.axis_size(axis)
    return lax.ppermute(value, axis, [(at, (at + steps) % count) for at in range(count)])


def from_all(value, axis):
    count = lax.axis_size(axis)
    return [value] + [turned(value, axis, step) for step in range(1, count)]


def summed_back(blocks, axis):
    total = blocks[0].astype(F32)
    for step in range(1, len(blocks)):
        total = total + turned(blocks[step], axis, -step).astype(F32)
    return total


def exchanged(blocks, axis):
    return lax.all_to_all(blocks, axis, 0, 0, tiled=True)


def lanes(columns):
    return pl.cdiv(columns, 128) * 128


def whole(array):
    return pl.BlockSpec(array.shape, lambda step: (0,) * len(array.shape))


SCALARS = pl.BlockSpec(memory_space=pltpu.SMEM)


def call(kernel, grid, in_specs, out_specs, out_shape, scratch, flops, moved, limit, *operands):
    return pl.pallas_call(
        kernel,
        grid=(grid,),
        in_specs=in_specs,
        out_specs=out_specs,
        out_shape=out_shape,
        scratch_shapes=scratch,
        compiler_params=pltpu.CompilerParams(vmem_limit_bytes=limit),
        cost_estimate=pl.CostEstimate(flops=flops, bytes_accessed=moved, transcendentals=0),
    )(*operands)


def block_forward_kernel(at, tokens, weights, hidden, slope):
    far = at[0]
    total = matmul(tokens[0], weights[far]) + matmul(tokens[1], weights[1 - far])
    act, rate = gelu_and_slope(total)
    columns = act.shape[1]
    hidden[...] = act.astype(BF16)
    slope[:, :columns] = rate.astype(BF16)
    if slope.shape[1] > columns:
        slope[:, columns:] = jnp.zeros((act.shape[0], slope.shape[1] - columns), BF16)


def block_forward(at, tokens, weights):
    parts, rows, width = tokens.shape
    columns = weights.shape[2]
    tile = rows // 4
    return call(
        block_forward_kernel,
        4,
        [
            SCALARS,
            pl.BlockSpec((parts, tile, width), lambda step: (0, step, 0)),
            whole(weights),
        ],
        [
            pl.BlockSpec((tile, columns), lambda step: (step, 0)),
            pl.BlockSpec((tile, lanes(columns)), lambda step: (step, 0)),
        ],
        [
            jax.ShapeDtypeStruct((rows, columns), BF16),
            jax.ShapeDtypeStruct((rows, lanes(columns)), BF16),
        ],
        [],
        2 * rows * columns * parts * width,
        2 * (parts * rows * width + parts * width * columns + 2 * rows * columns),
        LARGE,
        at,
        tokens,
        weights,
    )


def through_kernel(w_out, gated, out):
    n_near, n_images, part, _ = out.shape
    lat = gated.shape[1] // n_images
    total = matmul_tn(w_out[...], gated[...]).astype(BF16)
    for near in range(n_near):
        for image in range(n_images):
            for side in range(2):
                start = (2 * near + side) * part
                block = total[start : start + part, image * lat : (image + 1) * lat]
                out[near, image, :, side * lat : (side + 1) * lat] = block


def through_terms(w_out, gated, n_near, n_images):
    rows, columns = w_out.shape
    shape = (n_near, n_images, columns // (2 * n_near), 2 * gated.shape[1] // n_images)
    return call(
        through_kernel,
        1,
        [whole(w_out), whole(gated)],
        pl.BlockSpec(shape, lambda step: (0,) * len(shape)),
        jax.ShapeDtypeStruct(shape, BF16),
        [],
        2 * rows * columns * gated.shape[1],
        2 * rows * columns,
        LARGE,
        w_out,
        gated,
    )


def latent_kernel(at, hidden, terms, own_part, out, through, total):
    n_near, n_y, n_core, _, mine, _ = out.shape
    part, lat = terms.shape[1], through.shape[1]
    near, place = at[1], at[2]
    added = terms[0].astype(F32)
    for source in range(1, terms.shape[0]):
        added = added + terms[source].astype(F32)
    through[:part] = added[:, :lat].astype(BF16)
    through[part:] = added[:, lat:].astype(BF16)
    total[...] = matmul(hidden[...], through[...])
    rows = pl.ds(pl.multiple_of((place * n_near + near) * mine, mine), mine)
    total[rows] += own_part[pl.ds(pl.multiple_of(near * mine, mine), mine)]
    for y in range(n_y):
        for core in range(n_core):
            for side in range(n_near):
                start = ((y * n_core + core) * n_near + side) * mine
                block = total[start : start + mine].astype(BF16)
                for other in range(n_y):
                    out[side, other, core, y // 2, :, y % 2 * lat : (y % 2 + 1) * lat] = block


def latent_parts_of(at, hidden, terms, own_part, shape):
    rows, columns = hidden.shape
    lat = terms.shape[2] // 2
    return call(
        latent_kernel,
        1,
        [SCALARS, whole(hidden), whole(terms), whole(own_part)],
        [
            pl.BlockSpec(shape, lambda step: (0,) * len(shape)),
            pl.BlockSpec((columns, lat), lambda step: (0, 0)),
        ],
        [jax.ShapeDtypeStruct(shape, BF16), jax.ShapeDtypeStruct((columns, lat), BF16)],
        [pltpu.VMEM((rows, lat), F32)],
        2 * rows * columns * lat,
        2 * rows * columns,
        LARGE,
        at,
        hidden,
        terms,
        own_part,
    )


def inner_kernel(at, spread, hidden, grads, far_grads, inner):
    _, n_near, n_mp, mine, _ = spread.shape
    for image, result in ((at[0], grads), (1 - at[0], far_grads)):
        for place in range(n_mp):
            for near in range(n_near):
                start = (place * n_near + near) * mine
                result[start : start + mine] = spread[image, near, place]
    inner[...] = matmul_tn(grads[:, : inner.shape[0]], hidden[...]).astype(BF16)


def inner_products(at, spread, hidden, lat):
    rows, columns = hidden.shape
    shapes = [
        jax.ShapeDtypeStruct((rows, spread.shape[-1]), BF16),
        jax.ShapeDtypeStruct((rows, spread.shape[-1]), BF16),
        jax.ShapeDtypeStruct((lat, columns), BF16),
    ]
    return call(
        inner_kernel,
        1,
        [SCALARS, whole(spread), whole(hidden)],
        [whole(shape) for shape in shapes],
        shapes,
        [],
        2 * rows * columns * lat,
        2 * rows * columns,
        SMALL,
        at,
        spread,
        hidden,
    )


def block_backward_kernel(
    grads, through, slope, tokens, grads2, through2, slope2, tokens2, term, pre, pre2
):
    @pl.when(pl.program_id(0) == 0)
    def _():
        columns, lat = through.shape
        for grad, via, rate, result in (
            (grads, through, slope, pre),
            (grads2, through2, slope2, pre2),
        ):
            back = matmul_nt(grad[:, :lat], via[...])
            result[...] = (rate[:, :columns].astype(F32) * back).astype(BF16)

    total = matmul_tn(tokens[0], pre[...]) + matmul_tn(tokens2[...], pre2[...])
    term[...] = total.astype(BF16)


def block_backward(grads, through, slope, tokens, grads2, through2, slope2, tokens2):
    rows, width = tokens2.shape
    columns = through.shape[0]
    tile = min(640, width)
    return call(
        block_backward_kernel,
        pl.cdiv(width, tile),
        [
            whole(grads),
            whole(through),
            whole(slope),
            pl.BlockSpec((1, rows, tile), lambda step: (0, 0, step)),
            whole(grads2),
            whole(through2),
            whole(slope2),
            pl.BlockSpec((rows, tile), lambda step: (0, step)),
        ],
        pl.BlockSpec((tile, columns), lambda step: (step, 0)),
        jax.ShapeDtypeStruct((width, columns), BF16),
        [pltpu.VMEM((rows, columns), BF16)] * 2,
        4 * rows * columns * width,
        2 * (2 * rows * width + width * columns + 2 * rows * columns),
        LARGE,
        grads,
        through,
        slope,
        tokens,
        grads2,
        through2,
        slope2,
        tokens2,
    )


def decode_kernel(at, parts, w_dec1, w_dec2, w_patch, normed, embedded, slope, pixels, total, latent):
    step = pl.program_id(0)

    @pl.when(step == 0)
    def _():
        n_parts, pairs, mine, _ = parts.shape
        count = total.shape[0]
        lat = total.shape[2]
        added = parts[0].astype(F32)
        for source in range(1, n_parts):
            added = added + parts[source].astype(F32)
        for pair in range(pairs):
            total[2 * pair] = added[pair, :, :lat]
            total[2 * pair + 1] = added[pair, :, lat:]
        for turn in range(count):
            owner = lax.rem(at[3] - turn + count, count)
            latent[turn * mine : (turn + 1) * mine] = total[owner].astype(BF16)

    act, rate = silu_and_slope(matmul(latent[...], w_dec1[...]))
    slope[...] = rate[: slope.shape[0]]
    part = matmul(act.astype(BF16), w_dec2[...])

    @pl.when(step == 0)
    def _():
        pixels[...] = part

    @pl.when(step > 0)
    def _():
        pixels[...] += part

    @pl.when(step == pl.num_programs(0) - 1)
    def _():
        patches = matmul(pixels[...].astype(BF16), w_patch[...])
        normed[...] = layer_norm(patches).astype(BF16)
        embedded[...] = patches[: embedded.shape[0]]


def decode(at, parts, w_dec1, w_dec2, w_patch, mine):
    count, lat = 2 * parts.shape[1], parts.shape[3] // 2
    rows = count * mine
    deep, pix = w_dec2.shape
    width = w_patch.shape[1]
    tile = min(512, deep)
    return call(
        decode_kernel,
        deep // tile,
        [
            SCALARS,
            whole(parts),
            pl.BlockSpec((lat, tile), lambda step: (0, step)),
            pl.BlockSpec((tile, pix), lambda step: (step, 0)),
            whole(w_patch),
        ],
        [
            pl.BlockSpec((rows, width), lambda step: (0, 0)),
            pl.BlockSpec((mine, width), lambda step: (0, 0)),
            pl.BlockSpec((mine, tile), lambda step: (0, step)),
        ],
        [
            jax.ShapeDtypeStruct((rows, width), BF16),
            jax.ShapeDtypeStruct((mine, width), F32),
            jax.ShapeDtypeStruct((mine, deep), F32),
        ],
        [
            pltpu.VMEM((rows, pix), F32),
            pltpu.VMEM((count, mine, lat), F32),
            pltpu.VMEM((rows, lat), BF16),
        ],
        2 * rows * (lat * deep + deep * pix + pix * width),
        2 * (deep * pix + pix * width),
        SMALL,
        at,
        parts,
        w_dec1,
        w_dec2,
        w_patch,
    )


def reward_forward_kernel(normed, v1a, v1b, v2a, v2b, slope_a, slope_b, out, total):
    step = pl.program_id(0)
    part = 0.0
    for v1, v2, slope in ((v1a, v2a, slope_a), (v1b, v2b, slope_b)):
        act, rate = gelu_and_slope(matmul(normed[...], v1[...]))
        slope[...] = rate
        part = part + matmul(act.astype(BF16), v2[...])

    @pl.when(step == 0)
    def _():
        total[...] = part

    @pl.when(step > 0)
    def _():
        total[...] += part

    @pl.when(step == pl.num_programs(0) - 1)
    def _():
        out[...] = total[...].astype(BF16)


def reward_backward_kernel(grad, v1a, v1b, v2a, v2b, slope_a, slope_b, out, total):
    step = pl.program_id(0)
    part = 0.0
    for v1, v2, slope in ((v1a, v2a, slope_a), (v1b, v2b, slope_b)):
        back = (slope[...] * matmul_nt(grad[...], v2[...])).astype(BF16)
        part = part + matmul_nt(back, v1[...])

    @pl.when(step == 0)
    def _():
        total[...] = part

    @pl.when(step > 0)
    def _():
        total[...] += part

    @pl.when(step == pl.num_programs(0) - 1)
    def _():
        out[...] = total[...].astype(BF16)


def reward(values, v1_both, v2_both, slopes=None):
    rows, width = values.shape
    hidden = v1_both[0].shape[1]
    tile = hidden
    slope_spec = pl.BlockSpec((rows, tile), lambda step: (0, step))
    slope_shape = jax.ShapeDtypeStruct((rows, hidden), F32)
    out_spec = pl.BlockSpec((rows, width), lambda step: (0, 0))
    out_shape = jax.ShapeDtypeStruct((rows, width), BF16)
    v1_spec = pl.BlockSpec((width, tile), lambda step: (0, step))
    v2_spec = pl.BlockSpec((tile, width), lambda step: (step, 0))
    weight_specs = [whole(values), v1_spec, v1_spec, v2_spec, v2_spec]
    forward = slopes is None
    return call(
        reward_forward_kernel if forward else reward_backward_kernel,
        hidden // tile,
        weight_specs + ([] if forward else [slope_spec] * 2),
        [slope_spec] * 2 + [out_spec] if forward else out_spec,
        [slope_shape] * 2 + [out_shape] if forward else out_shape,
        [pltpu.VMEM((rows, width), F32)],
        8 * rows * width * hidden,
        8 * width * hidden,
        SMALL,
        values,
        *v1_both,
        *v2_both,
        *(() if forward else slopes),
    )


def on_device(
    latent_noise,
    timestep,
    reward_slot,
    target,
    modulation,
    w_in,
    w_out_t,
    w_final,
    w_dec1,
    w_dec2,
    w_patch,
    w_v1,
    w_v2,
):
    tok_dev = latent_noise.shape[1]
    n_near, n_y, n_core = (lax.axis_size(axis) for axis in TOKENS_AT)
    n_images = lax.axis_size("z") * lax.axis_size("far")
    n_rows = n_near * n_images
    n_tokens = n_near * n_y * n_core
    mine = tok_dev // n_near
    rows = tok_dev * n_y * n_core
    d_dev, ff_mp = w_in.shape
    width_d = d_dev * n_rows
    half = ff_mp // n_near
    lat = w_final.shape[1]
    scale = 1.0 / math.sqrt(n_images * rows)
    near = lax.axis_index("near")
    my_image = lax.axis_index(IMAGE)
    my_slot = reward_slot[my_image]

    n_z, n_far = lax.axis_size("z"), lax.axis_size("far")
    far = lax.axis_index("far")
    wide = width_d // n_far

    at = jnp.stack([far, near, lax.axis_index(("y", "core")), lax.axis_index("y")]).astype(jnp.int32)

    far_step = turned(timestep, "far", 1)
    pair_steps = jnp.where(far == 0, jnp.stack([timestep, far_step]), jnp.stack([far_step, timestep]))
    turned_steps = from_all(pair_steps, "z")

    split_in = jnp.moveaxis(w_in.reshape(d_dev, n_near, half), 1, 0)
    split_in = jnp.broadcast_to(split_in[None, :, None], (n_far, n_near, n_z, d_dev, half))
    split_in = split_in.reshape(n_rows, d_dev, half)
    split_in, turned_steps = lax.optimization_barrier((split_in, turned_steps))
    full_in = exchanged(split_in, FAR_FIRST).reshape(n_far, wide, half)

    noise_rows = latent_noise[0]
    modulate = modulation[timestep[0]]
    modulated = (
        layer_norm(noise_rows.astype(F32)) * (1.0 + modulate[1]) + modulate[0]
    ).astype(BF16)
    modulated = modulated.reshape(tok_dev, n_rows // n_far, n_far, d_dev)
    modulated = jnp.moveaxis(modulated, 2, 0).reshape(n_far, tok_dev, wide)
    modulated = jnp.where(far == 0, modulated, modulated[::-1])
    token_rows = lax.all_gather(modulated, ("y", "core"), axis=1, tiled=True)
    far_rows = lax.all_gather(turned(modulated[1], "far", 1), ("y", "core"), axis=0, tiled=True)

    all_steps = jnp.zeros((n_z, n_far), jnp.int32)
    for step, value in enumerate(turned_steps):
        owner = (lax.axis_index("z") - step) % n_z
        here = lax.broadcasted_iota(jnp.int32, (n_z, n_far), 0) == owner
        all_steps = jnp.where(here, value.reshape(1, n_far), all_steps)
    all_steps = all_steps.reshape(n_images)

    first = lax.axis_index(ROWS_AT) * d_dev
    my_final = lax.dynamic_slice_in_dim(w_final, first, d_dev, 0).astype(F32)
    gates = jnp.stack(
        [
            lax.dynamic_slice(modulation, (all_steps[image], 2, first), (1, 1, d_dev))[0, 0]
            for image in range(n_images)
        ]
    )
    gated = (gates.T[:, :, None] * my_final[:, None, :]).astype(BF16)
    terms = through_terms(w_out_t, gated.reshape(d_dev, n_images * lat), n_near, n_images)
    terms = terms.reshape((n_rows,) + terms.shape[2:])
    terms, full_in, own_target = lax.optimization_barrier((terms, full_in, target[0]))
    terms = exchanged(terms, ROWS_AT)

    v1_both = (w_v1, turned(w_v1, "core", 1))
    v2_both = (w_v2, turned(w_v2, "core", 1))

    hidden, hidden_slope = block_forward(at, token_rows, full_in)
    own_target = lax.dynamic_slice_in_dim(own_target, near * mine, mine, 0)
    own_target = jnp.pad(own_target, ((0, mine // 6), (0, 0)))
    goals = lax.all_gather(own_target, IMAGE, axis=0)
    goal = lax.dynamic_index_in_dim(goals, my_slot, 0, keepdims=False)[:mine]
    goal = goal.astype(F32)
    far_slope = turned(hidden_slope, "far", 1)
    own_part = matmul(noise_rows, w_final)
    shape = (n_near, n_y, n_core, n_y // 2, mine, 2 * lat)
    latent_part, through = latent_parts_of(at, hidden, terms, own_part, shape)
    far_through = turned(through, "far", 1)
    latent_parts = exchanged(latent_part.reshape(n_tokens, n_y // 2, mine, 2 * lat), TOKENS_AT)

    patch_rows, embedded, dec_slope = decode(at, latent_parts, w_dec1, w_dec2, w_patch, mine)
    *slopes, vit_part = reward(patch_rows, v1_both, v2_both)
    vit_out = summed_back(jnp.split(vit_part, n_y), "y")
    feature_grad = ((embedded + vit_out - goal) * scale).astype(BF16)

    grad_rows = jnp.concatenate(from_all(feature_grad, "y"))
    norm_part = reward(grad_rows, v1_both, v2_both, slopes)
    norm_grad = summed_back(jnp.split(norm_part, n_y), "y")
    norm_grad, far_slope, far_through = lax.optimization_barrier(
        (norm_grad, far_slope, far_through)
    )
    embed_grad = (feature_grad.astype(F32) + norm_back(embedded, norm_grad)).astype(BF16)
    pixel_grad = matmul_nt(embed_grad, w_patch).astype(BF16)
    dec_pre_grad = (dec_slope * matmul_nt(pixel_grad, w_dec2)).astype(BF16)
    latent_grad = matmul_nt(dec_pre_grad, w_dec1).astype(BF16)

    latent_grad = jnp.pad(latent_grad, ((0, 0), (0, lanes(lat) - lat)))
    spread = jnp.broadcast_to(latent_grad, (n_far * n_tokens,) + latent_grad.shape)
    spread = exchanged(spread, ("far",) + TOKENS_AT)
    spread = spread.reshape((n_far, n_near, n_y * n_core) + latent_grad.shape)

    latent_rows, far_latent_rows, inner = inner_products(at, spread, hidden, lat)
    far_inner = turned(inner, "far", 1)
    term_in = block_backward(
        latent_rows,
        through,
        hidden_slope,
        token_rows,
        far_latent_rows,
        far_through,
        far_slope,
        far_rows,
    )
    both = jnp.concatenate([inner, far_inner])
    both = jnp.broadcast_to(both, (n_near * n_z,) + both.shape)
    sent = jnp.concatenate([term_in.reshape(n_near * n_z, d_dev, half), both], axis=1)
    came = exchanged(sent, PAIR_ROWS).reshape(n_near, n_z, d_dev + 2 * lat, half)
    grad_in = jnp.sum(came[:, :, :d_dev].astype(F32), axis=1)
    grad_in = jnp.moveaxis(grad_in, 0, 1).reshape(d_dev, ff_mp)

    my_gated = gated.reshape(d_dev, n_z, n_far, lat)
    my_gated = jnp.where(far == 0, my_gated, my_gated[:, :, ::-1]).reshape(d_dev, n_images * lat)
    outs = [
        matmul(my_gated, came[at_near, :, d_dev:].reshape(n_images * lat, half))
        for at_near in range(n_near)
    ]
    return (grad_in, jnp.concatenate(outs, axis=1))


def solution(mesh):
    n_group, n_dp, n_mp = (mesh.shape[axis] for axis in ("group", "dp", "mp"))
    fine = Mesh(mesh.devices.reshape(n_group, n_dp // 2, 2, n_mp // 2, 2), AXES)
    tokens = ("y", "core")
    weights = P(ROWS_AT, tokens)
    placed = (
        P(IMAGE, tokens, None),
        P(IMAGE),
        P(),
        P(IMAGE, tokens, None),
        P(),
        weights,
        weights,
        P(),
        P(),
        P(),
        P(),
        P(None, tokens),
        P(tokens, None),
    )
    return jax.shard_map(
        on_device, mesh=fine, in_specs=placed, out_specs=(weights, weights), check_vma=False
    )
```

```python
import math

import jax
import jax.numpy as jnp
from jax import lax
from jax.experimental import pallas as pl
from jax.experimental.pallas import tpu as pltpu
from jax.sharding import Mesh
from jax.sharding import PartitionSpec as P

BF16 = jnp.bfloat16
GELU_SCALE = math.sqrt(2.0 / math.pi)
MIB = 1024 * 1024
SMALL, LARGE = 24 * MIB, 56 * MIB
F32 = jnp.float32
AXES = ("near", "z", "far", "y", "core")
IMAGE = ("z", "far")
ROWS_AT = ("near", "z", "far")
FAR_FIRST = ("far", "near", "z")
PAIR_ROWS = ("near", "z")
TOKENS_AT = ("near", "y", "core")


def layer_norm(values):
    mean = jnp.mean(values, axis=-1, keepdims=True)
    centred = values - mean
    variance = jnp.mean(centred * centred, axis=-1, keepdims=True)
    return centred * lax.rsqrt(variance + 1e-06)


def gelu_and_slope(values):
    inner = GELU_SCALE * (values + 0.044715 * values * values * values)
    bent = jnp.tanh(inner)
    half = 0.5 * (1.0 + bent)
    rate = GELU_SCALE * (1.0 + 3 * 0.044715 * values * values)
    return values * half, half + 0.5 * values * (1.0 - bent * bent) * rate


def silu_and_slope(values):
    gate = jax.nn.sigmoid(values)
    result = values * gate
    return result, gate + result * (1.0 - gate)


def norm_back(values, cotangent):
    _, pullback = jax.vjp(layer_norm, values)
    return pullback(cotangent)[0]


def matmul(left, right):
    return jnp.dot(left, right, preferred_element_type=F32)


def matmul_nt(left, right):
    return lax.dot_general(left, right, (((1,), (1,)), ((), ())), preferred_element_type=F32)


def matmul_tn(left, right):
    return lax.dot_general(left, right, (((0,), (0,)), ((), ())), preferred_element_type=F32)


def turned(value, axis, steps):
    count = lax.axis_size(axis)
    return lax.ppermute(value, axis, [(at, (at + steps) % count) for at in range(count)])


def from_all(value, axis):
    count = lax.axis_size(axis)
    return [value] + [turned(value, axis, step) for step in range(1, count)]


def summed_back(blocks, axis):
    total = blocks[0].astype(F32)
    for step in range(1, len(blocks)):
        total = total + turned(blocks[step], axis, -step).astype(F32)
    return total


def exchanged(blocks, axis):
    return lax.all_to_all(blocks, axis, 0, 0, tiled=True)


def lanes(columns):
    return pl.cdiv(columns, 128) * 128


def whole(array):
    return pl.BlockSpec(array.shape, lambda step: (0,) * len(array.shape))


SCALARS = pl.BlockSpec(memory_space=pltpu.SMEM)


def call(kernel, grid, in_specs, out_specs, out_shape, scratch, flops, moved, limit, *operands):
    return pl.pallas_call(
        kernel,
        grid=(grid,),
        in_specs=in_specs,
        out_specs=out_specs,
        out_shape=out_shape,
        scratch_shapes=scratch,
        compiler_params=pltpu.CompilerParams(vmem_limit_bytes=limit),
        cost_estimate=pl.CostEstimate(flops=flops, bytes_accessed=moved, transcendentals=0),
    )(*operands)


def block_forward_kernel(at, tokens, weights, hidden, slope):
    far = at[0]
    total = matmul(tokens[0], weights[far]) + matmul(tokens[1], weights[1 - far])
    act, rate = gelu_and_slope(total)
    columns = act.shape[1]
    hidden[...] = act.astype(BF16)
    slope[:, :columns] = rate.astype(BF16)
    if slope.shape[1] > columns:
        slope[:, columns:] = jnp.zeros((act.shape[0], slope.shape[1] - columns), BF16)


def block_forward(at, tokens, weights):
    parts, rows, width = tokens.shape
    columns = weights.shape[2]
    tile = rows // 4
    return call(
        block_forward_kernel,
        4,
        [
            SCALARS,
            pl.BlockSpec((parts, tile, width), lambda step: (0, step, 0)),
            whole(weights),
        ],
        [
            pl.BlockSpec((tile, columns), lambda step: (step, 0)),
            pl.BlockSpec((tile, lanes(columns)), lambda step: (step, 0)),
        ],
        [
            jax.ShapeDtypeStruct((rows, columns), BF16),
            jax.ShapeDtypeStruct((rows, lanes(columns)), BF16),
        ],
        [],
        2 * rows * columns * parts * width,
        2 * (parts * rows * width + parts * width * columns + 2 * rows * columns),
        LARGE,
        at,
        tokens,
        weights,
    )


def through_kernel(w_out, gated, out):
    n_near, n_images, part, _ = out.shape
    lat = gated.shape[1] // n_images
    total = matmul_tn(w_out[...], gated[...]).astype(BF16)
    for near in range(n_near):
        for image in range(n_images):
            for side in range(2):
                start = (2 * near + side) * part
                block = total[start : start + part, image * lat : (image + 1) * lat]
                out[near, image, :, side * lat : (side + 1) * lat] = block


def through_terms(w_out, gated, n_near, n_images):
    rows, columns = w_out.shape
    shape = (n_near, n_images, columns // (2 * n_near), 2 * gated.shape[1] // n_images)
    return call(
        through_kernel,
        1,
        [whole(w_out), whole(gated)],
        pl.BlockSpec(shape, lambda step: (0,) * len(shape)),
        jax.ShapeDtypeStruct(shape, BF16),
        [],
        2 * rows * columns * gated.shape[1],
        2 * rows * columns,
        LARGE,
        w_out,
        gated,
    )


def latent_kernel(at, hidden, terms, own_part, out, through, total):
    n_near, n_y, n_core, _, mine, _ = out.shape
    part, lat = terms.shape[1], through.shape[1]
    near, place = at[1], at[2]
    added = terms[0].astype(F32)
    for source in range(1, terms.shape[0]):
        added = added + terms[source].astype(F32)
    through[:part] = added[:, :lat].astype(BF16)
    through[part:] = added[:, lat:].astype(BF16)
    total[...] = matmul(hidden[...], through[...])
    rows = pl.ds(pl.multiple_of((place * n_near + near) * mine, mine), mine)
    total[rows] += own_part[pl.ds(pl.multiple_of(near * mine, mine), mine)]
    for y in range(n_y):
        for core in range(n_core):
            for side in range(n_near):
                start = ((y * n_core + core) * n_near + side) * mine
                block = total[start : start + mine].astype(BF16)
                for other in range(n_y):
                    out[side, other, core, y // 2, :, y % 2 * lat : (y % 2 + 1) * lat] = block


def latent_parts_of(at, hidden, terms, own_part, shape):
    rows, columns = hidden.shape
    lat = terms.shape[2] // 2
    return call(
        latent_kernel,
        1,
        [SCALARS, whole(hidden), whole(terms), whole(own_part)],
        [
            pl.BlockSpec(shape, lambda step: (0,) * len(shape)),
            pl.BlockSpec((columns, lat), lambda step: (0, 0)),
        ],
        [jax.ShapeDtypeStruct(shape, BF16), jax.ShapeDtypeStruct((columns, lat), BF16)],
        [pltpu.VMEM((rows, lat), F32)],
        2 * rows * columns * lat,
        2 * rows * columns,
        LARGE,
        at,
        hidden,
        terms,
        own_part,
    )


def inner_kernel(at, spread, hidden, grads, far_grads, inner):
    _, n_near, n_mp, mine, _ = spread.shape
    for image, result in ((at[0], grads), (1 - at[0], far_grads)):
        for place in range(n_mp):
            for near in range(n_near):
                start = (place * n_near + near) * mine
                result[start : start + mine] = spread[image, near, place]
    inner[...] = matmul_tn(grads[:, : inner.shape[0]], hidden[...]).astype(BF16)


def inner_products(at, spread, hidden, lat):
    rows, columns = hidden.shape
    shapes = [
        jax.ShapeDtypeStruct((rows, spread.shape[-1]), BF16),
        jax.ShapeDtypeStruct((rows, spread.shape[-1]), BF16),
        jax.ShapeDtypeStruct((lat, columns), BF16),
    ]
    return call(
        inner_kernel,
        1,
        [SCALARS, whole(spread), whole(hidden)],
        [whole(shape) for shape in shapes],
        shapes,
        [],
        2 * rows * columns * lat,
        2 * rows * columns,
        SMALL,
        at,
        spread,
        hidden,
    )


def block_backward_kernel(
    grads, through, slope, tokens, grads2, through2, slope2, tokens2, term, pre, pre2
):
    @pl.when(pl.program_id(0) == 0)
    def _():
        columns, lat = through.shape
        for grad, via, rate, result in (
            (grads, through, slope, pre),
            (grads2, through2, slope2, pre2),
        ):
            back = matmul_nt(grad[:, :lat], via[...])
            result[...] = (rate[:, :columns].astype(F32) * back).astype(BF16)

    total = matmul_tn(tokens[0], pre[...]) + matmul_tn(tokens2[...], pre2[...])
    term[...] = total.astype(BF16)


def block_backward(grads, through, slope, tokens, grads2, through2, slope2, tokens2):
    rows, width = tokens2.shape
    columns = through.shape[0]
    tile = min(640, width)
    return call(
        block_backward_kernel,
        pl.cdiv(width, tile),
        [
            whole(grads),
            whole(through),
            whole(slope),
            pl.BlockSpec((1, rows, tile), lambda step: (0, 0, step)),
            whole(grads2),
            whole(through2),
            whole(slope2),
            pl.BlockSpec((rows, tile), lambda step: (0, step)),
        ],
        pl.BlockSpec((tile, columns), lambda step: (step, 0)),
        jax.ShapeDtypeStruct((width, columns), BF16),
        [pltpu.VMEM((rows, columns), BF16)] * 2,
        4 * rows * columns * width,
        2 * (2 * rows * width + width * columns + 2 * rows * columns),
        LARGE,
        grads,
        through,
        slope,
        tokens,
        grads2,
        through2,
        slope2,
        tokens2,
    )


def decode_kernel(at, parts, w_dec1, w_dec2, w_patch, normed, embedded, slope, pixels, total, latent):
    step = pl.program_id(0)

    @pl.when(step == 0)
    def _():
        n_parts, pairs, mine, _ = parts.shape
        count = total.shape[0]
        lat = total.shape[2]
        added = parts[0].astype(F32)
        for source in range(1, n_parts):
            added = added + parts[source].astype(F32)
        for pair in range(pairs):
            total[2 * pair] = added[pair, :, :lat]
            total[2 * pair + 1] = added[pair, :, lat:]
        for turn in range(count):
            owner = lax.rem(at[3] - turn + count, count)
            latent[turn * mine : (turn + 1) * mine] = total[owner].astype(BF16)

    act, rate = silu_and_slope(matmul(latent[...], w_dec1[...]))
    slope[...] = rate[: slope.shape[0]]
    part = matmul(act.astype(BF16), w_dec2[...])

    @pl.when(step == 0)
    def _():
        pixels[...] = part

    @pl.when(step > 0)
    def _():
        pixels[...] += part

    @pl.when(step == pl.num_programs(0) - 1)
    def _():
        patches = matmul(pixels[...].astype(BF16), w_patch[...])
        normed[...] = layer_norm(patches).astype(BF16)
        embedded[...] = patches[: embedded.shape[0]]


def decode(at, parts, w_dec1, w_dec2, w_patch, mine):
    count, lat = 2 * parts.shape[1], parts.shape[3] // 2
    rows = count * mine
    deep, pix = w_dec2.shape
    width = w_patch.shape[1]
    tile = min(512, deep)
    return call(
        decode_kernel,
        deep // tile,
        [
            SCALARS,
            whole(parts),
            pl.BlockSpec((lat, tile), lambda step: (0, step)),
            pl.BlockSpec((tile, pix), lambda step: (step, 0)),
            whole(w_patch),
        ],
        [
            pl.BlockSpec((rows, width), lambda step: (0, 0)),
            pl.BlockSpec((mine, width), lambda step: (0, 0)),
            pl.BlockSpec((mine, tile), lambda step: (0, step)),
        ],
        [
            jax.ShapeDtypeStruct((rows, width), BF16),
            jax.ShapeDtypeStruct((mine, width), F32),
            jax.ShapeDtypeStruct((mine, deep), F32),
        ],
        [
            pltpu.VMEM((rows, pix), F32),
            pltpu.VMEM((count, mine, lat), F32),
            pltpu.VMEM((rows, lat), BF16),
        ],
        2 * rows * (lat * deep + deep * pix + pix * width),
        2 * (deep * pix + pix * width),
        SMALL,
        at,
        parts,
        w_dec1,
        w_dec2,
        w_patch,
    )


def reward_forward_kernel(normed, v1a, v1b, v2a, v2b, slope_a, slope_b, out, total):
    step = pl.program_id(0)
    part = 0.0
    for v1, v2, slope in ((v1a, v2a, slope_a), (v1b, v2b, slope_b)):
        act, rate = gelu_and_slope(matmul(normed[...], v1[...]))
        slope[...] = rate
        part = part + matmul(act.astype(BF16), v2[...])

    @pl.when(step == 0)
    def _():
        total[...] = part

    @pl.when(step > 0)
    def _():
        total[...] += part

    @pl.when(step == pl.num_programs(0) - 1)
    def _():
        out[...] = total[...].astype(BF16)


def reward_backward_kernel(grad, v1a, v1b, v2a, v2b, slope_a, slope_b, out, total):
    step = pl.program_id(0)
    part = 0.0
    for v1, v2, slope in ((v1a, v2a, slope_a), (v1b, v2b, slope_b)):
        back = (slope[...] * matmul_nt(grad[...], v2[...])).astype(BF16)
        part = part + matmul_nt(back, v1[...])

    @pl.when(step == 0)
    def _():
        total[...] = part

    @pl.when(step > 0)
    def _():
        total[...] += part

    @pl.when(step == pl.num_programs(0) - 1)
    def _():
        out[...] = total[...].astype(BF16)


def reward(values, v1_both, v2_both, slopes=None):
    rows, width = values.shape
    hidden = v1_both[0].shape[1]
    tile = hidden
    slope_spec = pl.BlockSpec((rows, tile), lambda step: (0, step))
    slope_shape = jax.ShapeDtypeStruct((rows, hidden), F32)
    out_spec = pl.BlockSpec((rows, width), lambda step: (0, 0))
    out_shape = jax.ShapeDtypeStruct((rows, width), BF16)
    v1_spec = pl.BlockSpec((width, tile), lambda step: (0, step))
    v2_spec = pl.BlockSpec((tile, width), lambda step: (step, 0))
    weight_specs = [whole(values), v1_spec, v1_spec, v2_spec, v2_spec]
    forward = slopes is None
    return call(
        reward_forward_kernel if forward else reward_backward_kernel,
        hidden // tile,
        weight_specs + ([] if forward else [slope_spec] * 2),
        [slope_spec] * 2 + [out_spec] if forward else out_spec,
        [slope_shape] * 2 + [out_shape] if forward else out_shape,
        [pltpu.VMEM((rows, width), F32)],
        8 * rows * width * hidden,
        8 * width * hidden,
        SMALL,
        values,
        *v1_both,
        *v2_both,
        *(() if forward else slopes),
    )


def on_device(
    latent_noise,
    timestep,
    reward_slot,
    target,
    modulation,
    w_in,
    w_out_t,
    w_final,
    w_dec1,
    w_dec2,
    w_patch,
    w_v1,
    w_v2,
):
    tok_dev = latent_noise.shape[1]
    n_near, n_y, n_core = (lax.axis_size(axis) for axis in TOKENS_AT)
    n_images = lax.axis_size("z") * lax.axis_size("far")
    n_rows = n_near * n_images
    n_tokens = n_near * n_y * n_core
    mine = tok_dev // n_near
    rows = tok_dev * n_y * n_core
    d_dev, ff_mp = w_in.shape
    width_d = d_dev * n_rows
    half = ff_mp // n_near
    lat = w_final.shape[1]
    scale = 1.0 / math.sqrt(n_images * rows)
    near = lax.axis_index("near")
    my_image = lax.axis_index(IMAGE)
    my_slot = reward_slot[my_image]

    n_z, n_far = lax.axis_size("z"), lax.axis_size("far")
    far = lax.axis_index("far")
    wide = width_d // n_far

    at = jnp.stack([far, near, lax.axis_index(("y", "core")), lax.axis_index("y")]).astype(jnp.int32)

    far_step = turned(timestep, "far", 1)
    pair_steps = jnp.where(far == 0, jnp.stack([timestep, far_step]), jnp.stack([far_step, timestep]))
    pair_steps, noise_rows = lax.optimization_barrier((pair_steps, latent_noise[0]))
    turned_steps = from_all(pair_steps, "z")

    split_in = jnp.moveaxis(w_in.reshape(d_dev, n_near, half), 1, 0)
    split_in = jnp.broadcast_to(split_in[None, :, None], (n_far, n_near, n_z, d_dev, half))
    split_in = split_in.reshape(n_rows, d_dev, half)
    split_in, turned_steps = lax.optimization_barrier((split_in, turned_steps))
    full_in = exchanged(split_in, FAR_FIRST).reshape(n_far, wide, half)

    modulate = modulation[timestep[0]]
    modulated = (
        layer_norm(noise_rows.astype(F32)) * (1.0 + modulate[1]) + modulate[0]
    ).astype(BF16)
    modulated = modulated.reshape(tok_dev, n_rows // n_far, n_far, d_dev)
    modulated = jnp.moveaxis(modulated, 2, 0).reshape(n_far, tok_dev, wide)
    modulated = jnp.where(far == 0, modulated, modulated[::-1])
    token_rows = lax.all_gather(modulated, ("y", "core"), axis=1, tiled=True)
    far_rows = lax.all_gather(turned(modulated[1], "far", 1), ("y", "core"), axis=0, tiled=True)

    all_steps = jnp.zeros((n_z, n_far), jnp.int32)
    for step, value in enumerate(turned_steps):
        owner = (lax.axis_index("z") - step) % n_z
        here = lax.broadcasted_iota(jnp.int32, (n_z, n_far), 0) == owner
        all_steps = jnp.where(here, value.reshape(1, n_far), all_steps)
    all_steps = all_steps.reshape(n_images)

    first = lax.axis_index(ROWS_AT) * d_dev
    my_final = lax.dynamic_slice_in_dim(w_final, first, d_dev, 0).astype(F32)
    gates = jnp.stack(
        [
            lax.dynamic_slice(modulation, (all_steps[image], 2, first), (1, 1, d_dev))[0, 0]
            for image in range(n_images)
        ]
    )
    gated = (gates.T[:, :, None] * my_final[:, None, :]).astype(BF16)
    terms = through_terms(w_out_t, gated.reshape(d_dev, n_images * lat), n_near, n_images)
    terms = terms.reshape((n_rows,) + terms.shape[2:])
    terms, full_in, own_target = lax.optimization_barrier((terms, full_in, target[0]))
    terms = exchanged(terms, ROWS_AT)

    v1_both = (w_v1, turned(w_v1, "core", 1))
    v2_both = (w_v2, turned(w_v2, "core", 1))

    hidden, hidden_slope = block_forward(at, token_rows, full_in)
    own_target = lax.dynamic_slice_in_dim(own_target, near * mine, mine, 0)
    own_target = jnp.pad(own_target, ((0, mine // 6), (0, 0)))
    goals = lax.all_gather(own_target, IMAGE, axis=0)
    goal = lax.dynamic_index_in_dim(goals, my_slot, 0, keepdims=False)[:mine]
    goal = goal.astype(F32)
    far_slope = turned(hidden_slope, "far", 1)
    own_part = matmul(noise_rows, w_final)
    shape = (n_near, n_y, n_core, n_y // 2, mine, 2 * lat)
    latent_part, through = latent_parts_of(at, hidden, terms, own_part, shape)
    far_through = turned(through, "far", 1)
    latent_parts = exchanged(latent_part.reshape(n_tokens, n_y // 2, mine, 2 * lat), TOKENS_AT)

    patch_rows, embedded, dec_slope = decode(at, latent_parts, w_dec1, w_dec2, w_patch, mine)
    *slopes, vit_part = reward(patch_rows, v1_both, v2_both)
    vit_out = summed_back(jnp.split(vit_part, n_y), "y")
    feature_grad = ((embedded + vit_out - goal) * scale).astype(BF16)

    grad_rows = jnp.concatenate(from_all(feature_grad, "y"))
    norm_part = reward(grad_rows, v1_both, v2_both, slopes)
    norm_grad = summed_back(jnp.split(norm_part, n_y), "y")
    norm_grad, far_slope, far_through = lax.optimization_barrier(
        (norm_grad, far_slope, far_through)
    )
    embed_grad = (feature_grad.astype(F32) + norm_back(embedded, norm_grad)).astype(BF16)
    pixel_grad = matmul_nt(embed_grad, w_patch).astype(BF16)
    dec_pre_grad = (dec_slope * matmul_nt(pixel_grad, w_dec2)).astype(BF16)
    latent_grad = matmul_nt(dec_pre_grad, w_dec1).astype(BF16)

    latent_grad = jnp.pad(latent_grad, ((0, 0), (0, lanes(lat) - lat)))
    spread = jnp.broadcast_to(latent_grad, (n_far * n_tokens,) + latent_grad.shape)
    spread = exchanged(spread, ("far",) + TOKENS_AT)
    spread = spread.reshape((n_far, n_near, n_y * n_core) + latent_grad.shape)

    latent_rows, far_latent_rows, inner = inner_products(at, spread, hidden, lat)
    far_inner = turned(inner, "far", 1)
    term_in = block_backward(
        latent_rows,
        through,
        hidden_slope,
        token_rows,
        far_latent_rows,
        far_through,
        far_slope,
        far_rows,
    )
    both = jnp.concatenate([inner, far_inner])
    both = jnp.broadcast_to(both, (n_near * n_z,) + both.shape)
    sent = jnp.concatenate([term_in.reshape(n_near * n_z, d_dev, half), both], axis=1)
    came = exchanged(sent, PAIR_ROWS).reshape(n_near, n_z, d_dev + 2 * lat, half)
    grad_in = jnp.sum(came[:, :, :d_dev].astype(F32), axis=1)
    grad_in = jnp.moveaxis(grad_in, 0, 1).reshape(d_dev, ff_mp)

    my_gated = gated.reshape(d_dev, n_z, n_far, lat)
    my_gated = jnp.where(far == 0, my_gated, my_gated[:, :, ::-1]).reshape(d_dev, n_images * lat)
    outs = [
        matmul(my_gated, came[at_near, :, d_dev:].reshape(n_images * lat, half))
        for at_near in range(n_near)
    ]
    return (grad_in, jnp.concatenate(outs, axis=1))


def solution(mesh):
    n_group, n_dp, n_mp = (mesh.shape[axis] for axis in ("group", "dp", "mp"))
    fine = Mesh(mesh.devices.reshape(n_group, n_dp // 2, 2, n_mp // 2, 2), AXES)
    tokens = ("y", "core")
    weights = P(ROWS_AT, tokens)
    placed = (
        P(IMAGE, tokens, None),
        P(IMAGE),
        P(),
        P(IMAGE, tokens, None),
        P(),
        weights,
        weights,
        P(),
        P(),
        P(),
        P(),
        P(None, tokens),
        P(tokens, None),
    )
    return jax.shard_map(
        on_device, mesh=fine, in_specs=placed, out_specs=(weights, weights), check_vma=False
    )
```
